32 devices in a mesh: grp: 4 (over z), exp: 4 (over y, x), rep: 2 (over core).
Axes of the slice: x: 2, y: 2, z: 4, core: 2. Of those that a mesh axis runs over, the one named last changes fastest.
Arguments:
- tokens: bfloat16 [1024, 2048], P(('grp', 'exp', 'rep')), may hold values from -6 to 6
- cotangent: bfloat16 [1024, 2048], P(('grp', 'exp', 'rep')), may hold values from -6 to 6
- expert_ids: int32 [1024, 8], P(('grp', 'exp', 'rep')), may hold values from 0 to 15, all different within a row; in each aligned block of 32 rows (0 to 31, 32 to 63, ...) at most 24 rows name the same one
- gate_probs: float32 [1024, 8], P(('grp', 'exp', 'rep')), may hold values from 0.05 to 0.6
- gate_weight: bfloat16 [16, 2048, 768], P(('grp', 'exp'), 'rep'), may hold values from -0.125 to 0.125
- up_weight: bfloat16 [16, 2048, 768], P(('grp', 'exp'), 'rep'), may hold values from -0.125 to 0.125
- down_weight: bfloat16 [16, 768, 2048], P(('grp', 'exp'), 'rep'), may hold values from -0.21875 to 0.21875
Outputs:
- layer_out: bfloat16 [1024, 2048], P(('grp', 'exp', 'rep'))
- token_grad: bfloat16 [1024, 2048], P(('grp', 'exp', 'rep'))
- gate_grad: bfloat16 [16, 2048, 768], P(('grp', 'exp'), 'rep')
- up_grad: bfloat16 [16, 2048, 768], P(('grp', 'exp'), 'rep')
- down_grad: bfloat16 [16, 768, 2048], P(('grp', 'exp'), 'rep')
The draws below stay inside these ranges and needn't reach their ends.
Inputs may be any that keep to these rules, and one draw needn't show every extreme that they name: `expert_ids`: each token names 8 different experts. Among the 32 tokens of one device, no expert is named more than 24 times, and in some device one expert is named exactly 24 times.
All inputs are finite; a program needn't handle non-finite values.
Results may differ from the reference program's by a relative error of at most 0.0065.
Values may be sent and summed in bfloat16 or wider, within the bound.
No kernel may reach another device: no remote copies, remote signals or barrier semaphores. Data moves between devices by JAX's collectives and lax.ppermute only.
A program may use at most 128 MiB of HBM per device.

```python
import math
import jax
import jax.numpy as jnp
import numpy as np
from jax import lax

D = 2048
FF = 768
TOP = 8
TOK_DEV = 32
EXPERTS = 16
TOKENS = 1024
CAP = 24
N_REP = 2


def shard_levels(key, extent, pieces, low, top_value):
    def one(dim, blocks):
        draws = jax.random.uniform(jax.random.fold_in(jax.random.fold_in(key, 6), dim), (blocks,), jnp.float32, low / len(pieces), top_value / len(pieces))
        return jnp.repeat(jnp.exp(draws), extent[dim] // blocks).reshape((-1,) + (1,) * (len(extent) - dim - 1))

    level = one(*pieces[0])
    for cut in pieces[1:]:
        level = level * one(*cut)
    return level


def assign_block(rng, own, number, rows, count, top, bound, skew):
    sequence = jax.random.permutation(rng, count)
    crowded, ordinary = shares(count, rows * top, bound, skew, True), shares(count, rows * top, bound, skew, False)
    places = jnp.arange(count)

    def named(lengths, offset_by):
        used = int((lengths > 0).sum())
        fixed = max(1, used // 4)
        shifted = fixed + (places - fixed + offset_by * (used - fixed)) % max(1, count - fixed)
        return jnp.zeros((count,), jnp.int32).at[sequence[jnp.where(places < fixed, places, shifted)]].set(jnp.asarray(lengths, jnp.int32))

    lengths = jnp.where(number % 4 == 0, named(crowded, number // 4), named(ordinary, number - number // 4 - 1))
    mixed = jax.random.permutation(jax.random.fold_in(own, 3), count)
    donor, sink = mixed[0:count // 2 * 2:2], mixed[1:count // 2 * 2:2]
    room = jnp.minimum(lengths[donor] - 1, bound - lengths[sink]) // 2
    room = jnp.where((donor == sequence[0]) | (sink == sequence[0]) | (lengths[sink] == 0), 0, jnp.maximum(room, 0))
    shifted = jax.random.randint(jax.random.fold_in(own, 4), (count // 2,), 0, 1 << 20) % (room + 1)
    lengths = lengths.at[donor].add(-shifted).at[sink].add(shifted)
    labels = jnp.searchsorted(jnp.cumsum(lengths), jnp.arange(rows * top), side="right").astype(jnp.int32)
    listing = labels.reshape(top, rows).T
    listing = listing[jax.random.permutation(jax.random.fold_in(own, 1), rows)]
    offset_by = jax.random.randint(jax.random.fold_in(own, 2), (rows, 1), 0, top)
    return jnp.take_along_axis(listing, (jnp.arange(top)[None, :] + offset_by) % top, axis=1)


def shares(number_of, total, reach, slope, full):
    portions = [(1 << 20) // math.isqrt(rank ** slope) + 1 for rank in range(1, number_of + 1)]
    largest = reach if full else min(reach, max(-(-total // number_of), total * portions[0] // sum(portions)))
    least = 1 if total - largest >= number_of - 1 else 0
    counts, rest = [largest] + [least] * (number_of - 1), total - largest - least * (number_of - 1)
    while rest > 0:
        free = [i for i in range(1, number_of) if counts[i] < largest] or [i for i in range(1, number_of) if counts[i] < reach]
        mass, left = sum([portions[i] for i in free]), rest
        for i in free:
            more = min(reach - counts[i], max(1, left * portions[i] // mass), rest)
            counts[i] = counts[i] + more
            rest = rest - more
    return np.array(counts)


def normal_values(rng, dims, deviation, limit, shards=(), held_as=jnp.bfloat16):
    gain = shard_levels(rng, dims, shards, -0.22, 0.18) if shards else 1.0
    result = jax.random.normal(rng, dims, jnp.float32) * deviation * gain
    return jnp.minimum(jnp.maximum(result, -limit), limit).astype(held_as)


def setup_inputs(seed: int = 0) -> dict:
    key_list = jax.random.split(jax.random.key(seed), 8)
    tokens = normal_values(key_list[0], (TOKENS, D), 1.0, 6.0, ((0, 32),))
    cotangent = normal_values(key_list[1], (TOKENS, D), 1.0, 6.0, ((0, 32),))
    expert_ids_keys = jax.random.split(jax.random.fold_in(key_list[2], 1), TOKENS // TOK_DEV)
    expert_ids_turns = jax.random.permutation(jax.random.fold_in(key_list[2], 3), TOKENS // TOK_DEV)
    expert_ids = jax.vmap(lambda own, number: assign_block(jax.random.fold_in(key_list[2], 2), own, number, TOK_DEV, EXPERTS, TOP, CAP, 2))(expert_ids_keys, expert_ids_turns).reshape((TOKENS, TOP))
    gate_probs = jnp.clip(jnp.exp(math.log(0.6) - 2.4849067 * jax.random.uniform(key_list[3], (TOKENS, TOP), jnp.float32) ** shard_levels(key_list[3], (TOKENS, TOP), ((0, 32),), -0.2, 0.2)), 0.05, 0.6)
    gate_weight = normal_values(key_list[4], (EXPERTS, D, FF), D ** -0.5, 0.125, ((0, 16), (1, 2)))
    up_weight = normal_values(key_list[5], (EXPERTS, D, FF), D ** -0.5, 0.125, ((0, 16), (1, 2)))
    down_weight = normal_values(key_list[6], (EXPERTS, FF, D), FF ** -0.5, 0.21875, ((0, 16), (1, 2)))
    return {"tokens": tokens, "cotangent": cotangent, "expert_ids": expert_ids, "gate_probs": gate_probs, "gate_weight": gate_weight, "up_weight": up_weight, "down_weight": down_weight}


def expert_pass(rows_in, rows_scaled, gate_mat, up_mat, down_mat):
    gate_pre = jnp.dot(rows_in, gate_mat, preferred_element_type=jnp.float32)
    up_pre = jnp.dot(rows_in, up_mat, preferred_element_type=jnp.float32)
    sigma = jax.nn.sigmoid(gate_pre)
    act = gate_pre * sigma
    hidden = (act * up_pre).astype(jnp.bfloat16)
    out_rows = jnp.dot(hidden, down_mat, preferred_element_type=jnp.float32).astype(jnp.bfloat16)
    dhidden = jnp.dot(rows_scaled, down_mat.T, preferred_element_type=jnp.float32)
    dgate = (dhidden * up_pre * sigma * (1.0 + gate_pre * (1.0 - sigma))).astype(jnp.bfloat16)
    dup = (dhidden * act).astype(jnp.bfloat16)
    grad_rows = (jnp.dot(dgate, gate_mat.T, preferred_element_type=jnp.float32)
                 + jnp.dot(dup, up_mat.T, preferred_element_type=jnp.float32)).astype(jnp.bfloat16)
    grad_gate = jnp.dot(rows_in.T, dgate, preferred_element_type=jnp.float32)
    grad_up = jnp.dot(rows_in.T, dup, preferred_element_type=jnp.float32)
    grad_down = jnp.dot(hidden.T, rows_scaled, preferred_element_type=jnp.float32)
    return out_rows, grad_rows, grad_gate, grad_up, grad_down


def reference(tokens, cotangent, expert_ids, gate_probs, gate_weight, up_weight, down_weight):
    row_count = TOKENS * TOP
    slot_count = EXPERTS * CAP
    flat_ids = expert_ids.reshape(row_count)
    flat_probs = gate_probs.reshape(row_count)
    row_token = jnp.arange(row_count, dtype=jnp.int32) // TOP
    row_replica = (row_token // TOK_DEV) % N_REP

    def per_expert(carry, expert):
        out_sum, grad_sum = carry
        totals = [jnp.zeros((D, FF), jnp.float32), jnp.zeros((D, FF), jnp.float32), jnp.zeros((FF, D), jnp.float32)]
        for replica in range(N_REP):
            chosen = (flat_ids == expert) & (row_replica == replica)
            index = jnp.nonzero(chosen, size=slot_count, fill_value=row_count)[0].astype(jnp.int32)
            token_index = (index // TOP).astype(jnp.int32)
            rows_in = jnp.take(tokens, token_index, axis=0, mode="fill", fill_value=0)
            rows_dy = jnp.take(cotangent, token_index, axis=0, mode="fill", fill_value=0)
            probs = jnp.take(flat_probs, index, mode="fill", fill_value=0)
            rows_scaled = (probs[:, None] * rows_dy.astype(jnp.float32)).astype(jnp.bfloat16)
            out_rows, grad_rows, grad_gate, grad_up, grad_down = expert_pass(
                rows_in, rows_scaled, gate_weight[expert], up_weight[expert], down_weight[expert])
            out_sum = out_sum.at[token_index].add(probs[:, None] * out_rows.astype(jnp.float32), mode="drop")
            grad_sum = grad_sum.at[token_index].add(grad_rows.astype(jnp.float32), mode="drop")
            partials = [grad_gate, grad_up, grad_down]
            for slot in range(3):
                rounded = lax.optimization_barrier(partials[slot].astype(jnp.bfloat16))
                totals[slot] = totals[slot] + rounded.astype(jnp.float32)
        return (out_sum, grad_sum), tuple(item.astype(jnp.bfloat16) for item in totals)

    start = (jnp.zeros((TOKENS, D), jnp.float32), jnp.zeros((TOKENS, D), jnp.float32))
    (out_sum, grad_sum), grads = lax.scan(per_expert, start, jnp.arange(EXPERTS, dtype=jnp.int32))
    return out_sum.astype(jnp.bfloat16), grad_sum.astype(jnp.bfloat16), grads[0], grads[1], grads[2]
```

```python
import jax
import jax.numpy as jnp
from jax import lax
from jax.sharding import PartitionSpec as P

TOP = 8


def partner_2(value, axis, bit):
    mask = 2**bit
    pairs = [(source, source ^ mask) for source in range(lax.axis_size(axis))]
    return lax.ppermute(value, axis, pairs)


def contract_rows(left, right):
    return lax.dot_general(
        left, right, (((0,), (0,)), ((), ())), preferred_element_type=jnp.float32
    )


def contract_cols(left, right):
    return lax.dot_general(
        left, right, (((1,), (1,)), ((), ())), preferred_element_type=jnp.float32
    )


def rounded_sum(first, second):
    left_part = lax.optimization_barrier(first.astype(jnp.bfloat16))
    right_part = lax.optimization_barrier(second.astype(jnp.bfloat16))
    return left_part.astype(jnp.float32) + right_part.astype(jnp.float32)


def routed_local(tokens, cotangent, expert_ids, gate_probs, gate_weight, up_weight, down_weight):
    group_count = lax.axis_size("grp")
    inner_count = lax.axis_size("exp")
    expert_count = group_count * inner_count
    token_count = tokens.shape[0]
    model_width = tokens.shape[1]
    capacity = 3 * token_count * TOP // (2 * expert_count)
    slot_count = expert_count * capacity
    row_count = token_count * TOP
    flat_ids = expert_ids.reshape(row_count)
    flat_probs = gate_probs.reshape(row_count)
    one_hot = (flat_ids[:, None] == jnp.arange(expert_count, dtype=jnp.int32)[None, :]).astype(
        jnp.float32
    )
    earlier = (jnp.arange(row_count)[:, None] > jnp.arange(row_count)[None, :]).astype(jnp.float32)
    counted = jnp.dot(earlier, one_hot, precision=lax.Precision.HIGHEST)
    slot_rank = jnp.sum(counted * one_hot, axis=1).astype(jnp.int32)
    target = flat_ids * capacity + slot_rank
    picked = jnp.arange(slot_count, dtype=jnp.int32)[:, None] == target[None, :]
    slot_probs = jnp.dot(picked.astype(jnp.float32), flat_probs, precision=lax.Precision.HIGHEST)
    pick_tokens = picked.reshape(slot_count, token_count, TOP).any(axis=2).astype(jnp.bfloat16)
    send_tokens = jnp.dot(pick_tokens, tokens, preferred_element_type=jnp.float32).astype(
        jnp.bfloat16
    )
    send_scaled = (
        jnp.dot(pick_tokens, cotangent, preferred_element_type=jnp.float32) * slot_probs[:, None]
    ).astype(jnp.bfloat16)
    whole = (
        lax.all_gather(gate_weight, "rep", axis=1, tiled=True),
        lax.all_gather(up_weight, "rep", axis=1, tiled=True),
        lax.all_gather(down_weight, "rep", axis=1, tiled=True),
    )
    gate_mat = whole[0][0]
    up_mat = whole[1][0]
    down_mat = whole[2][0]
    arrived = (
        lax.all_to_all(
            send_tokens.reshape(expert_count, capacity, model_width),
            ("grp", "exp"),
            split_axis=0,
            concat_axis=0,
            tiled=True,
        ),
        lax.all_to_all(
            send_scaled.reshape(expert_count, capacity, model_width),
            ("grp", "exp"),
            split_axis=0,
            concat_axis=0,
            tiled=True,
        ),
    )
    rows_in = arrived[0].reshape(slot_count, model_width)
    rows_scaled = arrived[1].reshape(slot_count, model_width)
    gate_pre = jnp.dot(rows_in, gate_mat, preferred_element_type=jnp.float32)
    up_pre = jnp.dot(rows_in, up_mat, preferred_element_type=jnp.float32)
    sigma = jax.nn.sigmoid(gate_pre)
    act = gate_pre * sigma
    hidden = (act * up_pre).astype(jnp.bfloat16)
    out_rows = jnp.dot(hidden, down_mat, preferred_element_type=jnp.float32).astype(jnp.bfloat16)
    dhidden = contract_cols(rows_scaled, down_mat)
    dgate = (dhidden * up_pre * sigma * (1.0 + gate_pre * (1.0 - sigma))).astype(jnp.bfloat16)
    dup = (dhidden * act).astype(jnp.bfloat16)
    grad_rows = (contract_cols(dgate, gate_mat) + contract_cols(dup, up_mat)).astype(jnp.bfloat16)
    returned = (
        lax.all_to_all(
            out_rows.reshape(expert_count, capacity, model_width),
            ("grp", "exp"),
            split_axis=0,
            concat_axis=0,
            tiled=True,
        ),
        lax.all_to_all(
            grad_rows.reshape(expert_count, capacity, model_width),
            ("grp", "exp"),
            split_axis=0,
            concat_axis=0,
            tiled=True,
        ),
    )
    replica = lax.axis_index("rep")
    other = 1 - replica
    half_width = gate_weight.shape[1]
    half_hidden = down_weight.shape[1]
    own_in = lax.dynamic_slice_in_dim(rows_in, replica * half_width, half_width, 1)
    own_hidden = lax.dynamic_slice_in_dim(hidden, replica * half_hidden, half_hidden, 1)
    send_in = lax.dynamic_slice_in_dim(rows_in, other * half_width, half_width, 1)
    send_hidden = lax.dynamic_slice_in_dim(hidden, other * half_hidden, half_hidden, 1)
    partner = partner_2((send_in, rows_scaled, send_hidden, dgate, dup), "rep", 0)
    gate_out = rounded_sum(contract_rows(own_in, dgate), contract_rows(partner[0], partner[3]))[
        None
    ]
    up_out = rounded_sum(contract_rows(own_in, dup), contract_rows(partner[0], partner[4]))[None]
    down_out = rounded_sum(
        contract_rows(own_hidden, rows_scaled), contract_rows(partner[2], partner[1])
    )[None]
    back_out = returned[0].reshape(slot_count, model_width)
    back_grad = returned[1].reshape(slot_count, model_width)
    route_out = jnp.dot(picked.T.astype(jnp.bfloat16), back_out, preferred_element_type=jnp.float32)
    layer_out = jnp.sum(
        route_out.reshape(token_count, TOP, model_width) * gate_probs[:, :, None], axis=1
    )
    token_grad = jnp.dot(pick_tokens.T, back_grad, preferred_element_type=jnp.float32)
    return (
        layer_out.astype(jnp.bfloat16),
        token_grad.astype(jnp.bfloat16),
        gate_out.astype(jnp.bfloat16),
        up_out.astype(jnp.bfloat16),
        down_out.astype(jnp.bfloat16),
    )


def shift_group(value, step):
    count = lax.axis_size("grp")
    return lax.ppermute(value, "grp", [(i, (i + step) % count) for i in range(count)])


def swap_inner(value, masks):
    inner, reps = lax.axis_size("exp"), lax.axis_size("rep")
    pairs = [
        (e * reps + r, (e ^ masks[r]) * reps + r) for e in range(inner) for r in range(reps)
    ]
    return lax.ppermute(value, ("exp", "rep"), pairs)


FIRST, SECOND = (1, 2), (2, 1)


def gather_blocks(block):
    count = lax.axis_size("grp")
    column = [block] + [shift_group(block, step) for step in range(1, count)]
    first = [swap_inner(piece, FIRST) for piece in column]
    second = [swap_inner(piece, SECOND) for piece in column]
    both = [swap_inner(piece, SECOND) for piece in first]
    return jnp.concatenate(column + first + second + both, axis=0)


def add_bf16(left, right):
    return (left.astype(jnp.float32) + right.astype(jnp.float32)).astype(jnp.bfloat16)


def reduce_blocks(rows, cuts):
    count = lax.axis_size("grp")
    width = rows.shape[1]
    blocks = rows.reshape(4, count, rows.shape[0] // (4 * count), width)
    part = count // cuts
    column = []
    for cut in range(cuts):
        here = blocks[:, cut * part : (cut + 1) * part]
        kept = add_bf16(here[:2], swap_inner(here[2:], SECOND))
        kept = add_bf16(kept[0], swap_inner(kept[1], FIRST))
        column += [kept[i] for i in range(part)]
    total = column[0].astype(jnp.float32)
    for step in range(1, count):
        total = total + shift_group(column[step], -step).astype(jnp.float32)
    return total.astype(jnp.bfloat16)


def route_weights(expert_ids, gate_probs, expert_count):
    group_count, inner_count = lax.axis_size("grp"), lax.axis_size("exp")
    named = expert_ids[None] == jnp.arange(expert_count, dtype=jnp.int32)[:, None, None]
    dense = jnp.sum(jnp.where(named, gate_probs[None], 0.0), axis=2)
    arrived = lax.all_to_all(dense, ("grp", "exp"), split_axis=0, concat_axis=0, tiled=True)
    group, inner, replica = lax.axis_index("grp"), lax.axis_index("exp"), lax.axis_index("rep")
    first = jnp.where(replica == 0, FIRST[0], FIRST[1])
    second = jnp.where(replica == 0, SECOND[0], SECOND[1])
    masks = jnp.stack([jnp.zeros_like(first), first, second, first ^ second])
    source = (
        jnp.mod(group - jnp.arange(group_count), group_count)[None, :] * inner_count
        + (inner ^ masks)[:, None]
    ).reshape(expert_count)
    picked = source[:, None] == jnp.arange(expert_count)[None, :]
    ordered = jnp.sum(jnp.where(picked[:, :, None], arrived[None], 0.0), axis=1)
    return ordered.reshape(expert_count * expert_ids.shape[0], 1)


def dense_local(tokens, cotangent, expert_ids, gate_probs, gate_weight, up_weight, down_weight):
    expert_count = lax.axis_size("grp") * lax.axis_size("exp")
    replica = lax.axis_index("rep")
    gate_mat = lax.all_gather(gate_weight, "rep", axis=1, tiled=True)[0]
    up_mat = lax.all_gather(up_weight, "rep", axis=1, tiled=True)[0]
    down_mat = lax.all_gather(down_weight, "rep", axis=1, tiled=True)[0]
    probs = route_weights(expert_ids, gate_probs, expert_count)
    rows_in = gather_blocks(tokens)
    rows_dy = gather_blocks(cotangent)
    gate_pre = jnp.dot(rows_in, gate_mat, preferred_element_type=jnp.float32)
    up_pre = jnp.dot(rows_in, up_mat, preferred_element_type=jnp.float32)
    sigma = jax.nn.sigmoid(gate_pre)
    act = gate_pre * sigma
    hidden = (act * up_pre).astype(jnp.bfloat16)
    out_rows = (jnp.dot(hidden, down_mat, preferred_element_type=jnp.float32) * probs).astype(
        jnp.bfloat16
    )
    layer_out = reduce_blocks(out_rows, 2)
    rows_scaled = (rows_dy.astype(jnp.float32) * probs).astype(jnp.bfloat16)
    dhidden = contract_cols(rows_scaled, down_mat)
    dgate = (dhidden * up_pre * sigma * (1.0 + gate_pre * (1.0 - sigma))).astype(jnp.bfloat16)
    dup = (dhidden * act).astype(jnp.bfloat16)
    grad_rows = (contract_cols(dgate, gate_mat) + contract_cols(dup, up_mat)).astype(jnp.bfloat16)
    token_grad = reduce_blocks(grad_rows, 2)
    half_width = gate_weight.shape[1]
    half_hidden = down_weight.shape[1]

    def half(value, which, size):
        return lax.dynamic_slice_in_dim(value, which * size, size, 1)

    other = 1 - replica
    sent = (
        contract_rows(half(rows_in, other, half_width), dgate).astype(jnp.bfloat16),
        contract_rows(half(rows_in, other, half_width), dup).astype(jnp.bfloat16),
        contract_rows(half(hidden, other, half_hidden), rows_scaled).astype(jnp.bfloat16),
    )
    partner = partner_2(sent, "rep", 0)
    gate_out = add_bf16(contract_rows(half(rows_in, replica, half_width), dgate), partner[0])
    up_out = add_bf16(contract_rows(half(rows_in, replica, half_width), dup), partner[1])
    down_out = add_bf16(contract_rows(half(hidden, replica, half_hidden), rows_scaled), partner[2])
    return layer_out, token_grad, gate_out[None], up_out[None], down_out[None]


def solution(mesh):
    in_specs = (
        P(("grp", "exp", "rep"), None),
        P(("grp", "exp", "rep"), None),
        P(("grp", "exp", "rep"), None),
        P(("grp", "exp", "rep"), None),
        P(("grp", "exp"), "rep", None),
        P(("grp", "exp"), "rep", None),
        P(("grp", "exp"), "rep", None),
    )
    out_specs = (
        P(("grp", "exp", "rep"), None),
        P(("grp", "exp", "rep"), None),
        P(("grp", "exp"), "rep", None),
        P(("grp", "exp"), "rep", None),
        P(("grp", "exp"), "rep", None),
    )
    sizes = dict(mesh.shape)
    whole_blocks = sizes["exp"] == 4 and sizes["rep"] == 2 and sizes["grp"] * sizes["exp"] <= 2 * TOP
    local = dense_local if whole_blocks else routed_local
    return jax.shard_map(local, mesh=mesh, in_specs=in_specs, out_specs=out_specs, check_vma=False)
```

```python
import functools

import jax
import jax.numpy as jnp
from jax import lax
from jax.experimental import pallas as pl
from jax.experimental.pallas import tpu as pltpu
from jax.sharding import PartitionSpec as P

TOP = 8


def partner_2(value, axis, bit):
    mask = 2**bit
    pairs = [(source, source ^ mask) for source in range(lax.axis_size(axis))]
    return lax.ppermute(value, axis, pairs)


def contract_rows(left, right):
    return lax.dot_general(
        left, right, (((0,), (0,)), ((), ())), preferred_element_type=jnp.float32
    )


def contract_cols(left, right):
    return lax.dot_general(
        left, right, (((1,), (1,)), ((), ())), preferred_element_type=jnp.float32
    )


def rounded_sum(first, second):
    left_part = lax.optimization_barrier(first.astype(jnp.bfloat16))
    right_part = lax.optimization_barrier(second.astype(jnp.bfloat16))
    return left_part.astype(jnp.float32) + right_part.astype(jnp.float32)


def routed_local(tokens, cotangent, expert_ids, gate_probs, gate_weight, up_weight, down_weight):
    group_count = lax.axis_size("grp")
    inner_count = lax.axis_size("exp")
    expert_count = group_count * inner_count
    token_count = tokens.shape[0]
    model_width = tokens.shape[1]
    capacity = 3 * token_count * TOP // (2 * expert_count)
    slot_count = expert_count * capacity
    row_count = token_count * TOP
    flat_ids = expert_ids.reshape(row_count)
    flat_probs = gate_probs.reshape(row_count)
    one_hot = (flat_ids[:, None] == jnp.arange(expert_count, dtype=jnp.int32)[None, :]).astype(
        jnp.float32
    )
    earlier = (jnp.arange(row_count)[:, None] > jnp.arange(row_count)[None, :]).astype(jnp.float32)
    counted = jnp.dot(earlier, one_hot, precision=lax.Precision.HIGHEST)
    slot_rank = jnp.sum(counted * one_hot, axis=1).astype(jnp.int32)
    target = flat_ids * capacity + slot_rank
    picked = jnp.arange(slot_count, dtype=jnp.int32)[:, None] == target[None, :]
    slot_probs = jnp.dot(picked.astype(jnp.float32), flat_probs, precision=lax.Precision.HIGHEST)
    pick_tokens = picked.reshape(slot_count, token_count, TOP).any(axis=2).astype(jnp.bfloat16)
    send_tokens = jnp.dot(pick_tokens, tokens, preferred_element_type=jnp.float32).astype(
        jnp.bfloat16
    )
    send_scaled = (
        jnp.dot(pick_tokens, cotangent, preferred_element_type=jnp.float32) * slot_probs[:, None]
    ).astype(jnp.bfloat16)
    whole = (
        lax.all_gather(gate_weight, "rep", axis=1, tiled=True),
        lax.all_gather(up_weight, "rep", axis=1, tiled=True),
        lax.all_gather(down_weight, "rep", axis=1, tiled=True),
    )
    gate_mat = whole[0][0]
    up_mat = whole[1][0]
    down_mat = whole[2][0]
    arrived = (
        lax.all_to_all(
            send_tokens.reshape(expert_count, capacity, model_width),
            ("grp", "exp"),
            split_axis=0,
            concat_axis=0,
            tiled=True,
        ),
        lax.all_to_all(
            send_scaled.reshape(expert_count, capacity, model_width),
            ("grp", "exp"),
            split_axis=0,
            concat_axis=0,
            tiled=True,
        ),
    )
    rows_in = arrived[0].reshape(slot_count, model_width)
    rows_scaled = arrived[1].reshape(slot_count, model_width)
    gate_pre = jnp.dot(rows_in, gate_mat, preferred_element_type=jnp.float32)
    up_pre = jnp.dot(rows_in, up_mat, preferred_element_type=jnp.float32)
    sigma = jax.nn.sigmoid(gate_pre)
    act = gate_pre * sigma
    hidden = (act * up_pre).astype(jnp.bfloat16)
    out_rows = jnp.dot(hidden, down_mat, preferred_element_type=jnp.float32).astype(jnp.bfloat16)
    dhidden = contract_cols(rows_scaled, down_mat)
    dgate = (dhidden * up_pre * sigma * (1.0 + gate_pre * (1.0 - sigma))).astype(jnp.bfloat16)
    dup = (dhidden * act).astype(jnp.bfloat16)
    grad_rows = (contract_cols(dgate, gate_mat) + contract_cols(dup, up_mat)).astype(jnp.bfloat16)
    returned = (
        lax.all_to_all(
            out_rows.reshape(expert_count, capacity, model_width),
            ("grp", "exp"),
            split_axis=0,
            concat_axis=0,
            tiled=True,
        ),
        lax.all_to_all(
            grad_rows.reshape(expert_count, capacity, model_width),
            ("grp", "exp"),
            split_axis=0,
            concat_axis=0,
            tiled=True,
        ),
    )
    replica = lax.axis_index("rep")
    other = 1 - replica
    half_width = gate_weight.shape[1]
    half_hidden = down_weight.shape[1]
    own_in = lax.dynamic_slice_in_dim(rows_in, replica * half_width, half_width, 1)
    own_hidden = lax.dynamic_slice_in_dim(hidden, replica * half_hidden, half_hidden, 1)
    send_in = lax.dynamic_slice_in_dim(rows_in, other * half_width, half_width, 1)
    send_hidden = lax.dynamic_slice_in_dim(hidden, other * half_hidden, half_hidden, 1)
    partner = partner_2((send_in, rows_scaled, send_hidden, dgate, dup), "rep", 0)
    gate_out = rounded_sum(contract_rows(own_in, dgate), contract_rows(partner[0], partner[3]))[
        None
    ]
    up_out = rounded_sum(contract_rows(own_in, dup), contract_rows(partner[0], partner[4]))[None]
    down_out = rounded_sum(
        contract_rows(own_hidden, rows_scaled), contract_rows(partner[2], partner[1])
    )[None]
    back_out = returned[0].reshape(slot_count, model_width)
    back_grad = returned[1].reshape(slot_count, model_width)
    route_out = jnp.dot(picked.T.astype(jnp.bfloat16), back_out, preferred_element_type=jnp.float32)
    layer_out = jnp.sum(
        route_out.reshape(token_count, TOP, model_width) * gate_probs[:, :, None], axis=1
    )
    token_grad = jnp.dot(pick_tokens.T, back_grad, preferred_element_type=jnp.float32)
    return (
        layer_out.astype(jnp.bfloat16),
        token_grad.astype(jnp.bfloat16),
        gate_out.astype(jnp.bfloat16),
        up_out.astype(jnp.bfloat16),
        down_out.astype(jnp.bfloat16),
    )


FIRST, SECOND = (1, 2), (2, 1)
VMEM_LIMIT = 56 * 2**20
ANY = pl.BlockSpec(memory_space=pl.ANY)
VMEM = pl.BlockSpec(memory_space=pltpu.VMEM)
SMEM = pl.BlockSpec(memory_space=pltpu.SMEM)


def shift_group(value, step):
    count = lax.axis_size("grp")
    return lax.ppermute(value, "grp", [(i, (i + step) % count) for i in range(count)])


def swap_inner(value, masks):
    inner, reps = lax.axis_size("exp"), lax.axis_size("rep")
    pairs = [
        (e * reps + r, (e ^ masks[r]) * reps + r) for e in range(inner) for r in range(reps)
    ]
    return lax.ppermute(value, ("exp", "rep"), pairs)


def steps_of(count):
    return [(q + 1) % count for q in range(count)]


def gather_blocks(block):
    count = lax.axis_size("grp")
    moved = {0: block, 1: shift_group(block, 1), count - 1: shift_group(block, -1)}
    for step in range(2, count - 1):
        moved[step] = shift_group(moved[step - 1], 1)
    column = [moved[step] for step in steps_of(count)]
    first = [swap_inner(piece, FIRST) for piece in column]
    second = [swap_inner(piece, SECOND) for piece in column]
    both = [swap_inner(piece, SECOND) for piece in first]
    return column + first + second + both


def add_bf16(left, right):
    return (left.astype(jnp.float32) + right.astype(jnp.float32)).astype(jnp.bfloat16)


def reduce_blocks(keep, sends, rows):
    count = lax.axis_size("grp")
    width = keep.shape[1]
    keep = keep.reshape(2, count * rows, width)
    part = count // len(sends) * rows
    column = []
    for cut, send in enumerate(sends):
        here = keep[:, cut * part : (cut + 1) * part]
        came = swap_inner(send, SECOND).reshape(2, part, width)
        passed = swap_inner(add_bf16(here[1], came[1]), FIRST)
        total = add_bf16(here[0].astype(jnp.float32) + came[0].astype(jnp.float32), passed)
        column += [total[i * rows : (i + 1) * rows] for i in range(part // rows)]
    total = column[-1].astype(jnp.float32)
    for piece, step in zip(column[:-1], steps_of(count)):
        total = total + shift_group(piece, -step).astype(jnp.float32)
    return total.astype(jnp.bfloat16)


def route_weights(expert_ids, gate_probs, expert_count):
    group_count, inner_count = lax.axis_size("grp"), lax.axis_size("exp")
    named = expert_ids[None] == jnp.arange(expert_count, dtype=jnp.int32)[:, None, None]
    dense = jnp.sum(jnp.where(named, gate_probs[None], 0.0), axis=2)
    arrived = lax.all_to_all(dense, ("grp", "exp"), split_axis=0, concat_axis=0, tiled=True)
    group, inner, replica = lax.axis_index("grp"), lax.axis_index("exp"), lax.axis_index("rep")
    first = jnp.where(replica == 0, FIRST[0], FIRST[1])
    second = jnp.where(replica == 0, SECOND[0], SECOND[1])
    masks = jnp.stack([jnp.zeros_like(first), first, second, first ^ second])
    steps = jnp.mod(jnp.arange(group_count) + 1, group_count)
    source = (
        jnp.mod(group - steps, group_count)[None, :] * inner_count + (inner ^ masks)[:, None]
    ).reshape(expert_count)
    picked = source[:, None] == jnp.arange(expert_count)[None, :]
    ordered = jnp.sum(jnp.where(picked[:, :, None], arrived[None], 0.0), axis=1)
    return ordered.reshape(expert_count * expert_ids.shape[0], 1)


def start_halves(halves, whole, sems, first_sem, replica):
    own, partner = halves
    size = own.shape[0]
    copies = []
    for k, (half, which) in enumerate(((own, replica), (partner, 1 - replica))):
        place = pl.ds(pl.multiple_of(which * size, size), size)
        copies.append(pltpu.make_async_copy(half, whole.at[place, :], sems.at[first_sem + k]))
        copies[-1].start()
    return copies


def start_rows(pieces, whole, offset, rows, sems):
    copies = []
    for k, piece in enumerate(pieces):
        copies.append(
            pltpu.make_async_copy(
                piece.at[pl.ds(offset, rows), :], whole.at[pl.ds(k * rows, rows), :], sems.at[k]
            )
        )
        copies[-1].start()
    return copies


def wait_all(copies):
    for copy in copies:
        copy.wait()


def tile_of(size, most=256):
    return most if size % most == 0 else size


def forward_kernel(rows, count, replica_ref, probs_ref, *refs):
    pieces, refs = refs[:count], refs[count:]
    gate, up, down = refs[0:2], refs[2:4], refs[4:6]
    keep_ref, send_ref, gate_pre_ref, up_pre_ref, hidden_ref, rows_ref = refs[6:12]
    gate_all, up_all, down_all, row_sems, weight_sems = refs[12:]
    replica = replica_ref[0]
    row_copies = start_rows(pieces, rows_ref, 0, rows, row_sems)
    gate_copies = start_halves(gate, gate_all, weight_sems, 0, replica)
    up_copies = start_halves(up, up_all, weight_sems, 2, replica)
    down_copies = start_halves(down, down_all, weight_sems, 4, replica)
    wait_all(row_copies + gate_copies + up_copies)
    tile = tile_of(gate_all.shape[1])

    @pl.loop(0, gate_all.shape[1] // tile)
    def _(i):
        cols = pl.ds(pl.multiple_of(i * tile, tile), tile)
        gate_pre = jnp.dot(rows_ref[...], gate_all[:, cols], preferred_element_type=jnp.float32)
        up_pre = jnp.dot(rows_ref[...], up_all[:, cols], preferred_element_type=jnp.float32)
        gate_pre_ref[:, cols] = gate_pre
        up_pre_ref[:, cols] = up_pre
        hidden_ref[:, cols] = (gate_pre * jax.nn.sigmoid(gate_pre) * up_pre).astype(jnp.bfloat16)

    wait_all(down_copies)
    half = keep_ref.shape[0]
    tile = tile_of(down_all.shape[1])

    @pl.loop(0, down_all.shape[1] // tile)
    def _(i):
        cols = pl.ds(pl.multiple_of(i * tile, tile), tile)
        out = jnp.dot(hidden_ref[...], down_all[:, cols], preferred_element_type=jnp.float32)
        out = (out * probs_ref[...]).astype(jnp.bfloat16)
        keep_ref[:, cols] = out[:half]
        send_ref[:, cols] = out[half:]


def backward_kernel(rows, count, replica_ref, probs_ref, gate_pre_ref, up_pre_ref, *refs):
    pieces, refs = refs[:count], refs[count:]
    gate, up, down = refs[0:2], refs[2:4], refs[4:6]
    keep_ref, near_ref, far_ref, dgate_ref, dup_ref, scaled_ref = refs[6:12]
    gate_all, up_all, down_all, row_sems, weight_sems = refs[12:]
    replica = replica_ref[0]
    row_copies = start_rows(pieces, scaled_ref, rows, rows, row_sems)
    down_copies = start_halves(down, down_all, weight_sems, 4, replica)
    gate_copies = start_halves(gate, gate_all, weight_sems, 0, replica)
    up_copies = start_halves(up, up_all, weight_sems, 2, replica)
    wait_all(row_copies)
    scaled_ref[...] = (scaled_ref[...].astype(jnp.float32) * probs_ref[...]).astype(jnp.bfloat16)
    wait_all(down_copies)
    tile = tile_of(down_all.shape[0])

    @pl.loop(0, down_all.shape[0] // tile)
    def _(i):
        cols = pl.ds(pl.multiple_of(i * tile, tile), tile)
        dhidden = contract_cols(scaled_ref[...], down_all[cols, :])
        gate_pre, up_pre = gate_pre_ref[:, cols], up_pre_ref[:, cols]
        sigma = jax.nn.sigmoid(gate_pre)
        dgate_ref[:, cols] = (
            dhidden * up_pre * sigma * (1.0 + gate_pre * (1.0 - sigma))
        ).astype(jnp.bfloat16)
        dup_ref[:, cols] = (dhidden * (gate_pre * sigma)).astype(jnp.bfloat16)

    wait_all(gate_copies + up_copies)
    half = keep_ref.shape[0]
    part = half // 4
    tile = tile_of(gate_all.shape[0])

    @pl.loop(0, gate_all.shape[0] // tile)
    def _(i):
        cols = pl.ds(pl.multiple_of(i * tile, tile), tile)
        grad = contract_cols(dgate_ref[...], gate_all[cols, :])
        grad = (grad + contract_cols(dup_ref[...], up_all[cols, :])).astype(jnp.bfloat16)
        keep_ref[:, cols] = grad[:half]
        for g in range(2):
            start = half + 2 * g * part
            near_ref[g * part : (g + 1) * part, cols] = grad[start : start + part]
            far_ref[g * part : (g + 1) * part, cols] = grad[start + part : start + 2 * part]


def expert_call(kernel, outs, width, hidden_width, count, total, matmuls, inputs, in_specs):
    return pl.pallas_call(
        kernel,
        out_shape=[jax.ShapeDtypeStruct(shape, dtype) for shape, dtype in outs],
        in_specs=in_specs,
        out_specs=[VMEM] * len(outs),
        scratch_shapes=[
            pltpu.VMEM((width, hidden_width), jnp.bfloat16),
            pltpu.VMEM((width, hidden_width), jnp.bfloat16),
            pltpu.VMEM((hidden_width, width), jnp.bfloat16),
            pltpu.SemaphoreType.DMA((count,)),
            pltpu.SemaphoreType.DMA((6,)),
        ],
        compiler_params=pltpu.CompilerParams(vmem_limit_bytes=VMEM_LIMIT),
        cost_estimate=pl.CostEstimate(
            flops=2 * matmuls * total * width * hidden_width,
            bytes_accessed=6 * width * hidden_width + 8 * total * width,
            transcendentals=total * hidden_width,
        ),
    )(*inputs)


def dense_local(tokens, cotangent, expert_ids, gate_probs, gate_weight, up_weight, down_weight):
    expert_count = lax.axis_size("grp") * lax.axis_size("exp")
    replica = lax.axis_index("rep")
    rows, width = tokens.shape
    half_width, hidden_width = gate_weight.shape[1:]
    half_hidden = down_weight.shape[1]
    total = expert_count * rows
    own = (gate_weight[0], up_weight[0], down_weight[0])
    partner = partner_2(own, "rep", 0)
    weights = [value for pair in zip(own, partner) for value in pair]
    probs = route_weights(expert_ids, gate_probs, expert_count)
    pieces = gather_blocks(jnp.concatenate([tokens, cotangent], axis=0))
    which = replica.astype(jnp.int32).reshape(1)
    bf16, f32 = jnp.bfloat16, jnp.float32
    out_keep, out_send, gate_pre, up_pre, hidden, rows_in = expert_call(
        functools.partial(forward_kernel, rows, expert_count),
        [
            ((total // 2, width), bf16),
            ((total // 2, width), bf16),
            ((total, hidden_width), f32),
            ((total, hidden_width), f32),
            ((total, hidden_width), bf16),
            ((total, width), bf16),
        ],
        width, hidden_width, expert_count, total, 3,
        [which, probs, *pieces, *weights],
        [SMEM, VMEM] + [ANY] * (expert_count + 6),
    )
    layer_out = reduce_blocks(out_keep, [out_send], rows)
    grad_keep, grad_near, grad_far, dgate, dup, rows_scaled = expert_call(
        functools.partial(backward_kernel, rows, expert_count),
        [
            ((total // 2, width), bf16),
            ((total // 4, width), bf16),
            ((total // 4, width), bf16),
            ((total, hidden_width), bf16),
            ((total, hidden_width), bf16),
            ((total, width), bf16),
        ],
        width, hidden_width, expert_count, total, 3,
        [which, probs, gate_pre, up_pre, *pieces, *weights],
        [SMEM, VMEM, VMEM, VMEM] + [ANY] * (expert_count + 6),
    )
    token_grad = reduce_blocks(grad_keep, [grad_near, grad_far], rows)

    def half(value, which, size):
        return lax.dynamic_slice_in_dim(value, which * size, size, 1)

    other = 1 - replica
    sent = (
        contract_rows(half(rows_in, other, half_width), dgate).astype(bf16),
        contract_rows(half(rows_in, other, half_width), dup).astype(bf16),
        contract_rows(half(hidden, other, half_hidden), rows_scaled).astype(bf16),
    )
    back = partner_2(sent, "rep", 0)
    gate_out = add_bf16(contract_rows(half(rows_in, replica, half_width), dgate), back[0])
    up_out = add_bf16(contract_rows(half(rows_in, replica, half_width), dup), back[1])
    down_out = add_bf16(contract_rows(half(hidden, replica, half_hidden), rows_scaled), back[2])
    return layer_out, token_grad, gate_out[None], up_out[None], down_out[None]


def solution(mesh):
    in_specs = (
        P(("grp", "exp", "rep"), None),
        P(("grp", "exp", "rep"), None),
        P(("grp", "exp", "rep"), None),
        P(("grp", "exp", "rep"), None),
        P(("grp", "exp"), "rep", None),
        P(("grp", "exp"), "rep", None),
        P(("grp", "exp"), "rep", None),
    )
    out_specs = (
        P(("grp", "exp", "rep"), None),
        P(("grp", "exp", "rep"), None),
        P(("grp", "exp"), "rep", None),
        P(("grp", "exp"), "rep", None),
        P(("grp", "exp"), "rep", None),
    )
    sizes = dict(mesh.shape)
    whole_blocks = sizes["exp"] == 4 and sizes["rep"] == 2 and sizes["grp"] * sizes["exp"] <= 2 * TOP
    local = dense_local if whole_blocks else routed_local
    return jax.shard_map(local, mesh=mesh, in_specs=in_specs, out_specs=out_specs, check_vma=False)
```

```python
import functools

import jax
import jax.numpy as jnp
from jax import lax
from jax.experimental import pallas as pl
from jax.experimental.pallas import tpu as pltpu
from jax.sharding import PartitionSpec as P

TOP = 8


def partner_2(value, axis, bit):
    mask = 2**bit
    pairs = [(source, source ^ mask) for source in range(lax.axis_size(axis))]
    return lax.ppermute(value, axis, pairs)


def contract_rows(left, right):
    return lax.dot_general(
        left, right, (((0,), (0,)), ((), ())), preferred_element_type=jnp.float32
    )


def contract_cols(left, right):
    return lax.dot_general(
        left, right, (((1,), (1,)), ((), ())), preferred_element_type=jnp.float32
    )


def rounded_sum(first, second):
    left_part = lax.optimization_barrier(first.astype(jnp.bfloat16))
    right_part = lax.optimization_barrier(second.astype(jnp.bfloat16))
    return left_part.astype(jnp.float32) + right_part.astype(jnp.float32)


def routed_local(tokens, cotangent, expert_ids, gate_probs, gate_weight, up_weight, down_weight):
    group_count = lax.axis_size("grp")
    inner_count = lax.axis_size("exp")
    expert_count = group_count * inner_count
    token_count = tokens.shape[0]
    model_width = tokens.shape[1]
    capacity = 3 * token_count * TOP // (2 * expert_count)
    slot_count = expert_count * capacity
    row_count = token_count * TOP
    flat_ids = expert_ids.reshape(row_count)
    flat_probs = gate_probs.reshape(row_count)
    one_hot = (flat_ids[:, None] == jnp.arange(expert_count, dtype=jnp.int32)[None, :]).astype(
        jnp.float32
    )
    earlier = (jnp.arange(row_count)[:, None] > jnp.arange(row_count)[None, :]).astype(jnp.float32)
    counted = jnp.dot(earlier, one_hot, precision=lax.Precision.HIGHEST)
    slot_rank = jnp.sum(counted * one_hot, axis=1).astype(jnp.int32)
    target = flat_ids * capacity + slot_rank
    picked = jnp.arange(slot_count, dtype=jnp.int32)[:, None] == target[None, :]
    slot_probs = jnp.dot(picked.astype(jnp.float32), flat_probs, precision=lax.Precision.HIGHEST)
    pick_tokens = picked.reshape(slot_count, token_count, TOP).any(axis=2).astype(jnp.bfloat16)
    send_tokens = jnp.dot(pick_tokens, tokens, preferred_element_type=jnp.float32).astype(
        jnp.bfloat16
    )
    send_scaled = (
        jnp.dot(pick_tokens, cotangent, preferred_element_type=jnp.float32) * slot_probs[:, None]
    ).astype(jnp.bfloat16)
    whole = (
        lax.all_gather(gate_weight, "rep", axis=1, tiled=True),
        lax.all_gather(up_weight, "rep", axis=1, tiled=True),
        lax.all_gather(down_weight, "rep", axis=1, tiled=True),
    )
    gate_mat = whole[0][0]
    up_mat = whole[1][0]
    down_mat = whole[2][0]
    arrived = (
        lax.all_to_all(
            send_tokens.reshape(expert_count, capacity, model_width),
            ("grp", "exp"),
            split_axis=0,
            concat_axis=0,
            tiled=True,
        ),
        lax.all_to_all(
            send_scaled.reshape(expert_count, capacity, model_width),
            ("grp", "exp"),
            split_axis=0,
            concat_axis=0,
            tiled=True,
        ),
    )
    rows_in = arrived[0].reshape(slot_count, model_width)
    rows_scaled = arrived[1].reshape(slot_count, model_width)
    gate_pre = jnp.dot(rows_in, gate_mat, preferred_element_type=jnp.float32)
    up_pre = jnp.dot(rows_in, up_mat, preferred_element_type=jnp.float32)
    sigma = jax.nn.sigmoid(gate_pre)
    act = gate_pre * sigma
    hidden = (act * up_pre).astype(jnp.bfloat16)
    out_rows = jnp.dot(hidden, down_mat, preferred_element_type=jnp.float32).astype(jnp.bfloat16)
    dhidden = contract_cols(rows_scaled, down_mat)
    dgate = (dhidden * up_pre * sigma * (1.0 + gate_pre * (1.0 - sigma))).astype(jnp.bfloat16)
    dup = (dhidden * act).astype(jnp.bfloat16)
    grad_rows = (contract_cols(dgate, gate_mat) + contract_cols(dup, up_mat)).astype(jnp.bfloat16)
    returned = (
        lax.all_to_all(
            out_rows.reshape(expert_count, capacity, model_width),
            ("grp", "exp"),
            split_axis=0,
            concat_axis=0,
            tiled=True,
        ),
        lax.all_to_all(
            grad_rows.reshape(expert_count, capacity, model_width),
            ("grp", "exp"),
            split_axis=0,
            concat_axis=0,
            tiled=True,
        ),
    )
    replica = lax.axis_index("rep")
    other = 1 - replica
    half_width = gate_weight.shape[1]
    half_hidden = down_weight.shape[1]
    own_in = lax.dynamic_slice_in_dim(rows_in, replica * half_width, half_width, 1)
    own_hidden = lax.dynamic_slice_in_dim(hidden, replica * half_hidden, half_hidden, 1)
    send_in = lax.dynamic_slice_in_dim(rows_in, other * half_width, half_width, 1)
    send_hidden = lax.dynamic_slice_in_dim(hidden, other * half_hidden, half_hidden, 1)
    partner = partner_2((send_in, rows_scaled, send_hidden, dgate, dup), "rep", 0)
    gate_out = rounded_sum(contract_rows(own_in, dgate), contract_rows(partner[0], partner[3]))[
        None
    ]
    up_out = rounded_sum(contract_rows(own_in, dup), contract_rows(partner[0], partner[4]))[None]
    down_out = rounded_sum(
        contract_rows(own_hidden, rows_scaled), contract_rows(partner[2], partner[1])
    )[None]
    back_out = returned[0].reshape(slot_count, model_width)
    back_grad = returned[1].reshape(slot_count, model_width)
    route_out = jnp.dot(picked.T.astype(jnp.bfloat16), back_out, preferred_element_type=jnp.float32)
    layer_out = jnp.sum(
        route_out.reshape(token_count, TOP, model_width) * gate_probs[:, :, None], axis=1
    )
    token_grad = jnp.dot(pick_tokens.T, back_grad, preferred_element_type=jnp.float32)
    return (
        layer_out.astype(jnp.bfloat16),
        token_grad.astype(jnp.bfloat16),
        gate_out.astype(jnp.bfloat16),
        up_out.astype(jnp.bfloat16),
        down_out.astype(jnp.bfloat16),
    )


FIRST, SECOND = (1, 2), (2, 1)
tie = lax.optimization_barrier
VMEM_LIMIT = 56 * 2**20
ANY = pl.BlockSpec(memory_space=pl.ANY)
SMEM = pl.BlockSpec(memory_space=pltpu.SMEM)


def swap_group(value, mask):
    count = lax.axis_size("grp")
    return lax.ppermute(value, "grp", [(i, i ^ mask) for i in range(count)])


def swap_inner(value, masks):
    inner, reps = lax.axis_size("exp"), lax.axis_size("rep")
    pairs = [
        (e * reps + r, (e ^ masks[r]) * reps + r) for e in range(inner) for r in range(reps)
    ]
    return lax.ppermute(value, ("exp", "rep"), pairs)


def steps_of(count):
    steps = [0]
    while len(steps) < count:
        steps = [2 * step for step in steps] + [2 * step + 1 for step in steps]
    return steps


def gather_blocks(block, beside):
    count = lax.axis_size("grp")
    beside, waiting = list(beside), list(range(len(beside)))
    moved, first, second, both = {0: block}, {}, {}, {}
    mask = 1
    while mask < count:
        moved[mask] = swap_group(block, mask)
        mask *= 2
    for k in range(count + 1):
        due = [
            (part, step)
            for part, step in ((moved, k), (first, k - 1), (second, k - 2), (both, k - 3))
            if k > 0 and step in part
        ]
        if k > 1 and waiting:
            due.append((beside, waiting.pop(0)))
        if due:
            for (part, step), value in zip(due, tie([part[step] for part, step in due])):
                part[step] = value
        if k < count:
            mask = 1
            while mask < (k & -k):
                moved[k | mask] = swap_group(moved[k], mask)
                mask *= 2
            first[k] = swap_inner(moved[k], FIRST)
            second[k] = swap_inner(moved[k], SECOND)
        if k > 0:
            both[k - 1] = swap_inner(first[k - 1], SECOND)
    pieces = [part[step] for part in (moved, first, second, both) for step in steps_of(count)]
    return pieces, beside


def add_bf16(left, right):
    return (left.astype(jnp.float32) + right.astype(jnp.float32)).astype(jnp.bfloat16)


def reduce_part(here, came):
    came = came.reshape(here.shape)
    passed = swap_inner(add_bf16(here[1], came[1]), FIRST)
    return add_bf16(here[0].astype(jnp.float32) + came[0].astype(jnp.float32), passed)


def reduce_column(column, beside=()):
    count = lax.axis_size("grp")
    rows = column.shape[0] // count
    came = [
        swap_group(column[q * rows : (q + 1) * rows], step)
        for q, step in enumerate(steps_of(count))
        if step
    ]
    came[0], *beside = tie((came[0], *beside)) if beside else came[:1]
    total = column[:rows].astype(jnp.float32)
    for value in came:
        total = total + value.astype(jnp.float32)
    return total.astype(jnp.bfloat16), beside


def token_block(tokens, cotangent, expert_ids, gate_probs, expert_count):
    named = expert_ids[:, :, None] == jnp.arange(expert_count, dtype=jnp.int32)
    rest = jnp.sum(jnp.where(named, gate_probs[:, :, None], 0.0), axis=1)
    terms = []
    for _ in range(3):
        terms.append(lax.reduce_precision(rest, exponent_bits=8, mantissa_bits=7))
        rest = rest - terms[-1]
    terms = jnp.concatenate(terms, axis=1).astype(jnp.bfloat16)
    rows, side = tokens.shape[0], side_width(expert_count)
    terms = jnp.pad(terms, ((0, rows), (0, side - terms.shape[1])))
    return jnp.concatenate([jnp.concatenate([tokens, cotangent], axis=0), terms], axis=1)


def side_width(expert_count):
    return -(-3 * expert_count // 128) * 128


def start_halves(halves, whole, sems, first_sem, replica):
    own, partner = halves
    size = own.shape[0]
    copies = []
    for k, (half, which) in enumerate(((own, replica), (partner, 1 - replica))):
        place = pl.ds(pl.multiple_of(which * size, size), size)
        copies.append(pltpu.make_async_copy(half, whole.at[place, :], sems.at[first_sem + k]))
        copies[-1].start()
    return copies


def start_rows(pieces, whole, offset, rows, first_col, sems):
    copies = []
    for k, piece in enumerate(pieces):
        part = piece.at[pl.ds(offset, rows), pl.ds(first_col, whole.shape[1])]
        copies.append(pltpu.make_async_copy(part, whole.at[pl.ds(k * rows, rows), :], sems.at[k]))
        copies[-1].start()
    return copies


def start_out(sources_and_places, sems, first_sem):
    copies = []
    for k, (source, place) in enumerate(sources_and_places):
        copies.append(pltpu.make_async_copy(source, place, sems.at[first_sem + k]))
        copies[-1].start()
    return copies


def wait_all(copies):
    for copy in copies:
        copy.wait()


def weights_of(side_ref, expert, expert_count):
    lane = lax.broadcasted_iota(jnp.int32, side_ref.shape, 1)
    mine = (lane == expert) | (lane == expert + expert_count) | (lane == expert + 2 * expert_count)
    return jnp.sum(jnp.where(mine, side_ref[...].astype(jnp.float32), 0.0), axis=1, keepdims=True)


def halves_of(whole, cols, keep, send):
    half = keep.shape[0]
    return [
        (whole.at[pl.ds(0, half), cols], keep.at[:, cols]),
        (whole.at[pl.ds(half, half), cols], send.at[:, cols]),
    ]


def tiles(size, count):
    return [pl.ds(i * size // count, size // count) for i in range(count)]


def forward_kernel(rows, count, where_ref, *refs):
    pieces, refs = refs[:count], refs[count:]
    gate, up, down = refs[0:2], refs[2:4], refs[4:6]
    keep, send, gate_pre_out, up_pre_out, hidden_out, rows_out = refs[6:12]
    rows_in, side, gate_all, up_all, down_all, gate_pre, up_pre, hidden, out = refs[12:21]
    row_sems, side_sems, weight_sems, out_sems = refs[21:]
    width = rows_in.shape[1]
    row_copies = start_rows(pieces, rows_in, 0, rows, 0, row_sems)
    gate_copies = start_halves(gate, gate_all, weight_sems, 0, where_ref[0])
    up_copies = start_halves(up, up_all, weight_sems, 2, where_ref[0])
    side_copies = start_rows(pieces, side, 0, rows, width, side_sems)
    down_copies = start_halves(down, down_all, weight_sems, 4, where_ref[0])
    wait_all(row_copies)
    outs = start_out([(rows_in, rows_out)], out_sems, 0)
    wait_all(gate_copies)
    gate_pre[...] = jnp.dot(rows_in[...], gate_all[...], preferred_element_type=jnp.float32)
    outs += start_out([(gate_pre, gate_pre_out)], out_sems, 1)
    wait_all(up_copies)
    up_pre[...] = jnp.dot(rows_in[...], up_all[...], preferred_element_type=jnp.float32)
    outs += start_out([(up_pre, up_pre_out)], out_sems, 2)
    act = gate_pre[...] * jax.nn.sigmoid(gate_pre[...])
    hidden[...] = (act * up_pre[...]).astype(jnp.bfloat16)
    outs += start_out([(hidden, hidden_out)], out_sems, 3)
    wait_all(side_copies)
    probs = weights_of(side, where_ref[1], count)
    wait_all(down_copies)
    for t, cols in enumerate(tiles(width, 2)):
        part = jnp.dot(hidden[...], down_all[:, cols], preferred_element_type=jnp.float32)
        out[:, cols] = (part * probs).astype(jnp.bfloat16)
        outs += start_out(halves_of(out, cols, keep, send), out_sems, 4 + 2 * t)
    wait_all(outs)


def backward_kernel(rows, count, where_ref, gate_pre_in, up_pre_in, *refs):
    pieces, refs = refs[:count], refs[count:]
    gate, up, down = refs[0:2], refs[2:4], refs[4:6]
    keep, send, dgate_out, dup_out, scaled_out = refs[6:11]
    scaled, side, gate_all, up_all, down_all, gate_pre, up_pre, dgate, dup, grad = refs[11:21]
    row_sems, side_sems, weight_sems, pre_sems, out_sems = refs[21:]
    width = scaled.shape[1]
    row_copies = start_rows(pieces, scaled, rows, rows, 0, row_sems)
    side_copies = start_rows(pieces, side, 0, rows, width, side_sems)
    down_copies = start_halves(down, down_all, weight_sems, 4, where_ref[0])
    pre_copies = start_out([(gate_pre_in, gate_pre), (up_pre_in, up_pre)], pre_sems, 0)
    gate_copies = start_halves(gate, gate_all, weight_sems, 0, where_ref[0])
    up_copies = start_halves(up, up_all, weight_sems, 2, where_ref[0])
    wait_all(row_copies + side_copies)
    probs = weights_of(side, where_ref[1], count)
    scaled[...] = (scaled[...].astype(jnp.float32) * probs).astype(jnp.bfloat16)
    outs = start_out([(scaled, scaled_out)], out_sems, 0)
    wait_all(down_copies)
    dhidden = contract_cols(scaled[...], down_all[...])
    wait_all(pre_copies)
    sigma = jax.nn.sigmoid(gate_pre[...])
    dgate[...] = (
        dhidden * up_pre[...] * sigma * (1.0 + gate_pre[...] * (1.0 - sigma))
    ).astype(jnp.bfloat16)
    dup[...] = (dhidden * (gate_pre[...] * sigma)).astype(jnp.bfloat16)
    outs += start_out([(dgate, dgate_out), (dup, dup_out)], out_sems, 1)
    wait_all(gate_copies + up_copies)
    for t, cols in enumerate(tiles(width, 2)):
        part = contract_cols(dgate[...], gate_all[cols, :])
        grad[:, cols] = (part + contract_cols(dup[...], up_all[cols, :])).astype(jnp.bfloat16)
        outs += start_out(halves_of(grad, cols, keep, send), out_sems, 3 + 2 * t)
    wait_all(outs)


def expert_call(kernel, outs, scratch, sems, flops, inputs):
    return pl.pallas_call(
        kernel,
        out_shape=[jax.ShapeDtypeStruct(shape, dtype) for shape, dtype in outs],
        in_specs=[SMEM] + [ANY] * (len(inputs) - 1),
        out_specs=[ANY] * len(outs),
        scratch_shapes=[pltpu.VMEM(shape, dtype) for shape, dtype in scratch]
        + [pltpu.SemaphoreType.DMA((n,)) for n in sems],
        compiler_params=pltpu.CompilerParams(vmem_limit_bytes=VMEM_LIMIT),
        cost_estimate=pl.CostEstimate(
            flops=flops,
            bytes_accessed=sum(2 * value.size for value in inputs),
            transcendentals=0,
        ),
    )(*inputs)


def partner_in_turn(values):
    came, values = [], list(values)
    for k in range(len(values)):
        came.append(partner_2(values[k], "rep", 0))
        if k + 1 < len(values):
            came[k], values[k + 1] = tie((came[k], values[k + 1]))
    return came


def dense_local(tokens, cotangent, expert_ids, gate_probs, gate_weight, up_weight, down_weight):
    expert_count = lax.axis_size("grp") * lax.axis_size("exp")
    replica = lax.axis_index("rep")
    rows, width = tokens.shape
    half_width, hidden_width = gate_weight.shape[1:]
    half_hidden = down_weight.shape[1]
    total = expert_count * rows
    own = (gate_weight[0], up_weight[0], down_weight[0])
    partner = partner_in_turn(own)
    block = token_block(tokens, cotangent, expert_ids, gate_probs, expert_count)
    pieces, partner = gather_blocks(block, partner)
    weights = [value for pair in zip(own, partner) for value in pair]
    expert = lax.axis_index("grp") * lax.axis_size("exp") + lax.axis_index("exp")
    where = jnp.stack([replica, expert]).astype(jnp.int32)
    bf16, f32 = jnp.bfloat16, jnp.float32
    wide, narrow, pre = ((total, width), bf16), ((total, hidden_width), bf16), ((total, hidden_width), f32)
    half_wide = ((total // 2, width), bf16)
    held = [
        wide,
        ((total, side_width(expert_count)), bf16),
        ((width, hidden_width), bf16),
        ((width, hidden_width), bf16),
        ((hidden_width, width), bf16),
        pre,
        pre,
    ]
    flops = 6 * total * width * hidden_width
    out_keep, out_send, gate_pre, up_pre, hidden, rows_in = expert_call(
        functools.partial(forward_kernel, rows, expert_count),
        [half_wide, half_wide, pre, pre, narrow, wide],
        held + [narrow, wide],
        [expert_count, expert_count, 6, 8],
        flops,
        [where, *pieces, *weights],
    )
    out_came = swap_inner(out_send, SECOND)
    grad_keep, grad_send, dgate, dup, rows_scaled = expert_call(
        functools.partial(backward_kernel, rows, expert_count),
        [half_wide, half_wide, narrow, narrow, wide],
        held + [narrow, narrow, wide],
        [expert_count, expert_count, 6, 2, 7],
        flops,
        [where, gate_pre, up_pre, *pieces, *weights],
    )
    out_came, grad_keep, grad_send, dgate, dup, rows_scaled = tie(
        (out_came, grad_keep, grad_send, dgate, dup, rows_scaled)
    )
    grad_came = swap_inner(grad_send, SECOND)
    out_column = reduce_part(out_keep.reshape(2, -1, width), out_came)
    grad_came, out_column, dgate, dup, rows_scaled, hidden, rows_in = tie(
        (grad_came, out_column, dgate, dup, rows_scaled, hidden, rows_in)
    )

    def half(value, which, size):
        return lax.dynamic_slice_in_dim(value, which * size, size, 1)

    other = 1 - replica
    sent = (
        contract_rows(half(rows_in, other, half_width), dgate).astype(bf16),
        contract_rows(half(rows_in, other, half_width), dup).astype(bf16),
        contract_rows(half(hidden, other, half_hidden), rows_scaled).astype(bf16),
    )
    back = partner_2(sent, "rep", 0)
    gate_out = add_bf16(contract_rows(half(rows_in, replica, half_width), dgate), back[0])
    up_out = add_bf16(contract_rows(half(rows_in, replica, half_width), dup), back[1])
    down_out = add_bf16(contract_rows(half(hidden, replica, half_hidden), rows_scaled), back[2])
    layer_out, _ = reduce_column(out_column)
    token_grad, (gate_out, up_out, down_out) = reduce_column(
        reduce_part(grad_keep.reshape(2, -1, width), grad_came), (gate_out, up_out, down_out)
    )
    return layer_out, token_grad, gate_out[None], up_out[None], down_out[None]


def solution(mesh):
    in_specs = (
        P(("grp", "exp", "rep"), None),
        P(("grp", "exp", "rep"), None),
        P(("grp", "exp", "rep"), None),
        P(("grp", "exp", "rep"), None),
        P(("grp", "exp"), "rep", None),
        P(("grp", "exp"), "rep", None),
        P(("grp", "exp"), "rep", None),
    )
    out_specs = (
        P(("grp", "exp", "rep"), None),
        P(("grp", "exp", "rep"), None),
        P(("grp", "exp"), "rep", None),
        P(("grp", "exp"), "rep", None),
        P(("grp", "exp"), "rep", None),
    )
    sizes = dict(mesh.shape)
    group_bits = sizes["grp"] & (sizes["grp"] - 1) == 0
    whole_blocks = sizes["exp"] == 4 and sizes["rep"] == 2 and group_bits and sizes["grp"] * sizes["exp"] <= 2 * TOP
    local = dense_local if whole_blocks else routed_local
    return jax.shard_map(local, mesh=mesh, in_specs=in_specs, out_specs=out_specs, check_vma=False)
```

```python
import functools

import jax
import jax.numpy as jnp
from jax import lax
from jax.experimental import pallas as pl
from jax.experimental.pallas import tpu as pltpu
from jax.sharding import PartitionSpec as P

TOP = 8


def partner_2(value, axis, bit):
    mask = 2**bit
    pairs = [(source, source ^ mask) for source in range(lax.axis_size(axis))]
    return lax.ppermute(value, axis, pairs)


def contract_rows(left, right):
    return lax.dot_general(
        left, right, (((0,), (0,)), ((), ())), preferred_element_type=jnp.float32
    )


def contract_cols(left, right):
    return lax.dot_general(
        left, right, (((1,), (1,)), ((), ())), preferred_element_type=jnp.float32
    )


def rounded_sum(first, second):
    left_part = lax.optimization_barrier(first.astype(jnp.bfloat16))
    right_part = lax.optimization_barrier(second.astype(jnp.bfloat16))
    return left_part.astype(jnp.float32) + right_part.astype(jnp.float32)


def routed_local(tokens, cotangent, expert_ids, gate_probs, gate_weight, up_weight, down_weight):
    group_count = lax.axis_size("grp")
    inner_count = lax.axis_size("exp")
    expert_count = group_count * inner_count
    token_count = tokens.shape[0]
    model_width = tokens.shape[1]
    capacity = 3 * token_count * TOP // (2 * expert_count)
    slot_count = expert_count * capacity
    row_count = token_count * TOP
    flat_ids = expert_ids.reshape(row_count)
    flat_probs = gate_probs.reshape(row_count)
    one_hot = (flat_ids[:, None] == jnp.arange(expert_count, dtype=jnp.int32)[None, :]).astype(
        jnp.float32
    )
    earlier = (jnp.arange(row_count)[:, None] > jnp.arange(row_count)[None, :]).astype(jnp.float32)
    counted = jnp.dot(earlier, one_hot, precision=lax.Precision.HIGHEST)
    slot_rank = jnp.sum(counted * one_hot, axis=1).astype(jnp.int32)
    target = flat_ids * capacity + slot_rank
    picked = jnp.arange(slot_count, dtype=jnp.int32)[:, None] == target[None, :]
    slot_probs = jnp.dot(picked.astype(jnp.float32), flat_probs, precision=lax.Precision.HIGHEST)
    pick_tokens = picked.reshape(slot_count, token_count, TOP).any(axis=2).astype(jnp.bfloat16)
    send_tokens = jnp.dot(pick_tokens, tokens, preferred_element_type=jnp.float32).astype(
        jnp.bfloat16
    )
    send_scaled = (
        jnp.dot(pick_tokens, cotangent, preferred_element_type=jnp.float32) * slot_probs[:, None]
    ).astype(jnp.bfloat16)
    whole = (
        lax.all_gather(gate_weight, "rep", axis=1, tiled=True),
        lax.all_gather(up_weight, "rep", axis=1, tiled=True),
        lax.all_gather(down_weight, "rep", axis=1, tiled=True),
    )
    gate_mat = whole[0][0]
    up_mat = whole[1][0]
    down_mat = whole[2][0]
    arrived = (
        lax.all_to_all(
            send_tokens.reshape(expert_count, capacity, model_width),
            ("grp", "exp"),
            split_axis=0,
            concat_axis=0,
            tiled=True,
        ),
        lax.all_to_all(
            send_scaled.reshape(expert_count, capacity, model_width),
            ("grp", "exp"),
            split_axis=0,
            concat_axis=0,
            tiled=True,
        ),
    )
    rows_in = arrived[0].reshape(slot_count, model_width)
    rows_scaled = arrived[1].reshape(slot_count, model_width)
    gate_pre = jnp.dot(rows_in, gate_mat, preferred_element_type=jnp.float32)
    up_pre = jnp.dot(rows_in, up_mat, preferred_element_type=jnp.float32)
    sigma = jax.nn.sigmoid(gate_pre)
    act = gate_pre * sigma
    hidden = (act * up_pre).astype(jnp.bfloat16)
    out_rows = jnp.dot(hidden, down_mat, preferred_element_type=jnp.float32).astype(jnp.bfloat16)
    dhidden = contract_cols(rows_scaled, down_mat)
    dgate = (dhidden * up_pre * sigma * (1.0 + gate_pre * (1.0 - sigma))).astype(jnp.bfloat16)
    dup = (dhidden * act).astype(jnp.bfloat16)
    grad_rows = (contract_cols(dgate, gate_mat) + contract_cols(dup, up_mat)).astype(jnp.bfloat16)
    returned = (
        lax.all_to_all(
            out_rows.reshape(expert_count, capacity, model_width),
            ("grp", "exp"),
            split_axis=0,
            concat_axis=0,
            tiled=True,
        ),
        lax.all_to_all(
            grad_rows.reshape(expert_count, capacity, model_width),
            ("grp", "exp"),
            split_axis=0,
            concat_axis=0,
            tiled=True,
        ),
    )
    replica = lax.axis_index("rep")
    other = 1 - replica
    half_width = gate_weight.shape[1]
    half_hidden = down_weight.shape[1]
    own_in = lax.dynamic_slice_in_dim(rows_in, replica * half_width, half_width, 1)
    own_hidden = lax.dynamic_slice_in_dim(hidden, replica * half_hidden, half_hidden, 1)
    send_in = lax.dynamic_slice_in_dim(rows_in, other * half_width, half_width, 1)
    send_hidden = lax.dynamic_slice_in_dim(hidden, other * half_hidden, half_hidden, 1)
    partner = partner_2((send_in, rows_scaled, send_hidden, dgate, dup), "rep", 0)
    gate_out = rounded_sum(contract_rows(own_in, dgate), contract_rows(partner[0], partner[3]))[
        None
    ]
    up_out = rounded_sum(contract_rows(own_in, dup), contract_rows(partner[0], partner[4]))[None]
    down_out = rounded_sum(
        contract_rows(own_hidden, rows_scaled), contract_rows(partner[2], partner[1])
    )[None]
    back_out = returned[0].reshape(slot_count, model_width)
    back_grad = returned[1].reshape(slot_count, model_width)
    route_out = jnp.dot(picked.T.astype(jnp.bfloat16), back_out, preferred_element_type=jnp.float32)
    layer_out = jnp.sum(
        route_out.reshape(token_count, TOP, model_width) * gate_probs[:, :, None], axis=1
    )
    token_grad = jnp.dot(pick_tokens.T, back_grad, preferred_element_type=jnp.float32)
    return (
        layer_out.astype(jnp.bfloat16),
        token_grad.astype(jnp.bfloat16),
        gate_out.astype(jnp.bfloat16),
        up_out.astype(jnp.bfloat16),
        down_out.astype(jnp.bfloat16),
    )


FIRST, SECOND = (1, 2), (2, 1)
tie = lax.optimization_barrier
VMEM_LIMIT = 56 * 2**20
ANY = pl.BlockSpec(memory_space=pl.ANY)
SMEM = pl.BlockSpec(memory_space=pltpu.SMEM)


def swap_group(value, mask):
    count = lax.axis_size("grp")
    return lax.ppermute(value, "grp", [(i, i ^ mask) for i in range(count)])


def swap_inner(value, masks):
    inner, reps = lax.axis_size("exp"), lax.axis_size("rep")
    pairs = [
        (e * reps + r, (e ^ masks[r]) * reps + r) for e in range(inner) for r in range(reps)
    ]
    return lax.ppermute(value, ("exp", "rep"), pairs)


def steps_of(count):
    steps = [0]
    while len(steps) < count:
        steps = [2 * step for step in steps] + [2 * step + 1 for step in steps]
    return steps


def gather_blocks(block, beside):
    count = lax.axis_size("grp")
    moved, first, second, both = {0: block, 1: swap_group(block, 1)}, {}, {}, {}
    for k in range(count + 1):
        due = [
            (part, step)
            for part, step in ((moved, k), (first, k - 1), (second, k - 1), (both, k - 3))
            if k > 0 and step in part
        ]
        values = beside(k, [part[step] for part, step in due])
        for (part, step), value in zip(due, values):
            part[step] = value
        if k == 0:
            mask = 2
            while mask < count:
                moved[mask] = swap_group(moved[0], mask)
                mask *= 2
        if k < count:
            mask = 1
            while mask < (k & -k):
                moved[k | mask] = swap_group(moved[k], mask)
                mask *= 2
            first[k] = swap_inner(moved[k], FIRST)
            second[k] = swap_inner(moved[k], SECOND)
        if k > 0:
            both[k - 1] = swap_inner(first[k - 1], SECOND)
    return [part[step] for part in (moved, first, second, both) for step in steps_of(count)]


def add_bf16(left, right):
    return (left.astype(jnp.float32) + right.astype(jnp.float32)).astype(jnp.bfloat16)


def reduce_part(here, came):
    came = came.reshape(here.shape)
    passed = swap_inner(add_bf16(here[1], came[1]), FIRST)
    return add_bf16(here[0].astype(jnp.float32) + came[0].astype(jnp.float32), passed)


def send_column(column):
    count = lax.axis_size("grp")
    rows = column.shape[0] // count
    return [
        column[q * rows : (q + 1) * rows] if step == 0
        else swap_group(column[q * rows : (q + 1) * rows], step)
        for q, step in enumerate(steps_of(count))
    ]


def halve_column(column, masks):
    for mask in masks:
        half = column.shape[0] // 2
        column = add_bf16(column[:half], swap_group(column[half:], mask))
    return column


def add_all(values):
    total = values[0].astype(jnp.float32)
    for value in values[1:]:
        total = total + value.astype(jnp.float32)
    return total.astype(jnp.bfloat16)


def token_block(tokens, cotangent, expert_ids, gate_probs, expert_count):
    named = expert_ids[:, :, None] == jnp.arange(expert_count, dtype=jnp.int32)
    rest = jnp.sum(jnp.where(named, gate_probs[:, :, None], 0.0), axis=1)
    terms = []
    for _ in range(3):
        terms.append(lax.reduce_precision(rest, exponent_bits=8, mantissa_bits=7))
        rest = rest - terms[-1]
    terms = jnp.concatenate(terms, axis=1).astype(jnp.bfloat16)
    rows, side = tokens.shape[0], side_width(expert_count)
    terms = jnp.pad(terms, ((0, rows), (0, side - terms.shape[1])))
    return jnp.concatenate([jnp.concatenate([tokens, cotangent], axis=0), terms], axis=1)


def side_width(expert_count):
    return -(-3 * expert_count // 128) * 128


def start_halves(halves, whole, sems, first_sem, replica):
    own, partner = halves
    size = own.shape[0]
    copies = []
    for k, (half, which) in enumerate(((own, replica), (partner, 1 - replica))):
        place = pl.ds(pl.multiple_of(which * size, size), size)
        copies.append(pltpu.make_async_copy(half, whole.at[place, :], sems.at[first_sem + k]))
        copies[-1].start()
    return copies


def start_rows(pieces, whole, offset, rows, first_col, sems):
    copies = []
    for k, piece in enumerate(pieces):
        part = piece.at[pl.ds(offset, rows), pl.ds(first_col, whole.shape[1])]
        copies.append(pltpu.make_async_copy(part, whole.at[pl.ds(k * rows, rows), :], sems.at[k]))
        copies[-1].start()
    return copies


def start_out(sources_and_places, sems, first_sem):
    copies = []
    for k, (source, place) in enumerate(sources_and_places):
        copies.append(pltpu.make_async_copy(source, place, sems.at[first_sem + k]))
        copies[-1].start()
    return copies


def start_parts(parts, whole, sems, first_sem):
    size = parts[0].shape[0]
    places = [whole.at[pl.ds(k * size, size), :] for k in range(len(parts))]
    return start_out(list(zip(parts, places)), sems, first_sem)


def wait_all(copies):
    for copy in copies:
        copy.wait()


def weights_of(side_ref, expert, expert_count):
    lane = lax.broadcasted_iota(jnp.int32, side_ref.shape, 1)
    mine = (lane == expert) | (lane == expert + expert_count) | (lane == expert + 2 * expert_count)
    return jnp.sum(jnp.where(mine, side_ref[...].astype(jnp.float32), 0.0), axis=1, keepdims=True)


def halves_of(whole, cols, keep, send):
    half = keep.shape[0]
    return [
        (whole.at[pl.ds(0, half), cols], keep.at[:, cols]),
        (whole.at[pl.ds(half, half), cols], send.at[:, cols]),
    ]


def tiles(size, count):
    return [pl.ds(i * size // count, size // count) for i in range(count)]


def assemble_kernel(rows, count, *refs):
    pieces, halves, refs = refs[:count], refs[count : count + 2], refs[count + 2 :]
    whole_out, hidden_out, whole, hidden, sems, half_sems, out_sems = refs
    copies = start_rows(pieces, whole, 0, rows, 0, sems)
    wait_all(copies + start_parts(halves, hidden, half_sems, 0))
    wait_all(start_out([(whole, whole_out), (hidden, hidden_out)], out_sems, 0))


def forward_kernel(rows, count, expert_count, where_ref, *refs):
    pieces, refs = refs[:count], refs[count:]
    gate, up, down = refs[0:2], refs[2:4], refs[4:6]
    whole_out, gate_pre_out, up_pre_out, hidden_out = refs[6:10]
    rows_in, side, gate_all, up_all, down_all, gate_pre, up_pre, hidden, out = refs[10:19]
    row_sems, side_sems, weight_sems, out_sems = refs[19:]
    width = rows_in.shape[1]
    row_copies = start_rows(pieces, rows_in, 0, rows, 0, row_sems)
    gate_copies = start_halves(gate, gate_all, weight_sems, 0, where_ref[0])
    wait_all(row_copies)
    up_copies = start_halves(up, up_all, weight_sems, 2, where_ref[0])
    wait_all(gate_copies)
    side_copies = start_rows(pieces, side, 0, rows, width, side_sems)
    down_copies = start_halves(down, down_all, weight_sems, 4, where_ref[0])
    pre = jnp.dot(rows_in[...], gate_all[...], preferred_element_type=jnp.float32)
    gate_pre[...] = pre.astype(gate_pre.dtype)
    act = pre * jax.nn.sigmoid(pre)
    wait_all(up_copies)
    pre = jnp.dot(rows_in[...], up_all[...], preferred_element_type=jnp.float32)
    up_pre[...] = pre.astype(up_pre.dtype)
    hidden[...] = (act * pre).astype(jnp.bfloat16)
    outs = start_out(
        [(gate_pre, gate_pre_out), (up_pre, up_pre_out), (hidden, hidden_out)], out_sems, 0
    )
    wait_all(side_copies)
    probs = weights_of(side, where_ref[1], expert_count)
    wait_all(down_copies)
    for t, cols in enumerate(tiles(width, 2)):
        part = jnp.dot(hidden[...], down_all[:, cols], preferred_element_type=jnp.float32)
        out[:, cols] = (part * probs).astype(jnp.bfloat16)
        outs += start_out([(out.at[:, cols], whole_out.at[:, cols])], out_sems, 3 + t)
    wait_all(outs)


def backward_kernel(rows, count, where_ref, *refs):
    gate_pre_in, up_pre_in, refs = refs[0:2], refs[2:4], refs[4:]
    pieces, refs = refs[:count], refs[count:]
    gate, up, down = refs[0:2], refs[2:4], refs[4:6]
    keep, send, dgate_out, dup_out, scaled_out = refs[6:11]
    scaled, side, gate_all, up_all, down_all, gate_pre, up_pre, dgate, dup, grad = refs[11:21]
    row_sems, side_sems, weight_sems, pre_sems, out_sems = refs[21:]
    width = scaled.shape[1]
    row_copies = start_rows(pieces, scaled, rows, rows, 0, row_sems)
    side_copies = start_rows(pieces, side, 0, rows, width, side_sems)
    down_copies = start_halves(down, down_all, weight_sems, 4, where_ref[0])
    pre_copies = start_parts(gate_pre_in, gate_pre, pre_sems, 0)
    pre_copies += start_parts(up_pre_in, up_pre, pre_sems, 2)
    wait_all(row_copies + side_copies)
    gate_copies = start_halves(gate, gate_all, weight_sems, 0, where_ref[0])
    up_copies = start_halves(up, up_all, weight_sems, 2, where_ref[0])
    probs = weights_of(side, where_ref[1], count)
    scaled[...] = (scaled[...].astype(jnp.float32) * probs).astype(jnp.bfloat16)
    outs = start_out([(scaled, scaled_out)], out_sems, 0)
    wait_all(down_copies)
    dhidden = contract_cols(scaled[...], down_all[...])
    wait_all(pre_copies)
    pre, gain = gate_pre[...].astype(jnp.float32), up_pre[...].astype(jnp.float32)
    sigma = jax.nn.sigmoid(pre)
    dgate[...] = (dhidden * gain * sigma * (1.0 + pre * (1.0 - sigma))).astype(jnp.bfloat16)
    dup[...] = (dhidden * (pre * sigma)).astype(jnp.bfloat16)
    outs += start_out([(dgate, dgate_out), (dup, dup_out)], out_sems, 1)
    wait_all(gate_copies + up_copies)
    for t, cols in enumerate(tiles(width, 2)):
        part = contract_cols(dgate[...], gate_all[cols, :])
        grad[:, cols] = (part + contract_cols(dup[...], up_all[cols, :])).astype(jnp.bfloat16)
        outs += start_out(halves_of(grad, cols, keep, send), out_sems, 3 + 2 * t)
    wait_all(outs)


def expert_call(kernel, outs, scratch, sems, flops, inputs):
    return pl.pallas_call(
        kernel,
        out_shape=[jax.ShapeDtypeStruct(shape, dtype) for shape, dtype in outs],
        in_specs=[SMEM] + [ANY] * (len(inputs) - 1),
        out_specs=[ANY] * len(outs),
        scratch_shapes=[pltpu.VMEM(shape, dtype) for shape, dtype in scratch]
        + [pltpu.SemaphoreType.DMA((n,)) for n in sems],
        compiler_params=pltpu.CompilerParams(vmem_limit_bytes=VMEM_LIMIT),
        cost_estimate=pl.CostEstimate(
            flops=flops,
            bytes_accessed=sum(2 * value.size for value in inputs),
            transcendentals=0,
        ),
    )(*inputs)


class PartnerWeights:
    def __init__(self, own):
        self.own, self.came = list(own), []

    def __call__(self, step, values):
        if not values:
            return values
        k = len(self.came)
        old, new = self.came[k - 1 :] if k > 1 else [], self.own[k : k + 1]
        values = list(tie((*values, *old, *new)))
        if new:
            self.came.append(partner_2(values.pop(), "rep", 0))
        if old:
            self.came[k - 1] = values.pop()
        return values


def dense_local(tokens, cotangent, expert_ids, gate_probs, gate_weight, up_weight, down_weight):
    expert_count = lax.axis_size("grp") * lax.axis_size("exp")
    replica = lax.axis_index("rep")
    rows, width = tokens.shape
    half_width, hidden_width = gate_weight.shape[1:]
    half_hidden = down_weight.shape[1]
    total = expert_count * rows
    own = (gate_weight[0], up_weight[0], down_weight[0])
    partner = PartnerWeights(own)
    block = token_block(tokens, cotangent, expert_ids, gate_probs, expert_count)
    pieces = gather_blocks(block, partner)
    partner = partner.came
    weights = [value for pair in zip(own, partner) for value in pair]
    expert = lax.axis_index("grp") * lax.axis_size("exp") + lax.axis_index("exp")
    where = jnp.stack([replica, expert]).astype(jnp.int32)
    bf16 = jnp.bfloat16
    wide, narrow = ((total, width), bf16), ((total, hidden_width), bf16)
    half_wide = ((total // 2, width), bf16)
    half_narrow = ((total // 2, hidden_width), bf16)
    mats = [
        ((width, hidden_width), bf16),
        ((width, hidden_width), bf16),
        ((hidden_width, width), bf16),
    ]
    side = side_width(expert_count)
    flops = 6 * total * width * hidden_width
    half_count = expert_count // 2
    forward, waiting = [], pieces[half_count:]
    for half_pieces in (pieces[:half_count], None):
        forward.append(
            list(expert_call(
                functools.partial(forward_kernel, rows, half_count, expert_count),
                [half_wide] + [half_narrow] * 3,
                [half_wide, ((total // 2, side), bf16), *mats] + [half_narrow] * 3 + [half_wide],
                [half_count, half_count, 6, 5],
                flops // 2,
                [where, *(half_pieces or waiting), *weights],
            ))
        )
        if half_pieces:
            forward[0][0], waiting = tie((forward[0][0], waiting))
    (out_keep, out_send), gate_pre, up_pre, hidden = zip(*forward)
    held = [wide, ((total, side), bf16), *mats, narrow, narrow]
    out_came = swap_inner(out_send, SECOND)
    rows_in, hidden = pl.pallas_call(
        functools.partial(assemble_kernel, rows, expert_count),
        out_shape=[jax.ShapeDtypeStruct(*wide), jax.ShapeDtypeStruct(*narrow)],
        in_specs=[ANY] * (expert_count + 2),
        out_specs=[ANY, ANY],
        scratch_shapes=[
            pltpu.VMEM(*wide),
            pltpu.VMEM(*narrow),
            pltpu.SemaphoreType.DMA((expert_count,)),
            pltpu.SemaphoreType.DMA((2,)),
            pltpu.SemaphoreType.DMA((2,)),
        ],
        compiler_params=pltpu.CompilerParams(vmem_limit_bytes=VMEM_LIMIT // 4),
    )(*pieces, *hidden)
    grad_keep, grad_send, dgate, dup, rows_scaled = expert_call(
        functools.partial(backward_kernel, rows, expert_count),
        [half_wide, half_wide, narrow, narrow, wide],
        held + [narrow, narrow, wide],
        [expert_count, expert_count, 6, 4, 7],
        flops,
        [where, *gate_pre, *up_pre, *pieces, *weights],
    )
    out_came, grad_keep, grad_send, dgate, dup, rows_scaled = tie(
        (out_came, grad_keep, grad_send, dgate, dup, rows_scaled)
    )
    grad_came = swap_inner(grad_send, SECOND)
    out_column = reduce_part(out_keep.reshape(2, -1, width), out_came)
    grad_came, out_column, dgate, dup, rows_scaled, hidden, rows_in = tie(
        (grad_came, out_column, dgate, dup, rows_scaled, hidden, rows_in)
    )

    def half(value, which, size):
        return lax.dynamic_slice_in_dim(value, which * size, size, 1)

    other = 1 - replica
    sent = (
        contract_rows(half(rows_in, other, half_width), dgate).astype(bf16),
        contract_rows(half(rows_in, other, half_width), dup).astype(bf16),
        contract_rows(half(hidden, other, half_hidden), rows_scaled).astype(bf16),
    )
    back = partner_2(sent, "rep", 0)
    gate_out = add_bf16(contract_rows(half(rows_in, replica, half_width), dgate), back[0])
    up_out = add_bf16(contract_rows(half(rows_in, replica, half_width), dup), back[1])
    down_out = add_bf16(contract_rows(half(hidden, replica, half_hidden), rows_scaled), back[2])
    masks = [2**bit for bit in range(lax.axis_size("grp").bit_length() - 1)]
    out_column = halve_column(out_column, masks[:-1])
    half = out_column.shape[0] // 2
    out_terms = [out_column[:half], swap_group(out_column[half:], masks[-1])]
    grad_column = reduce_part(grad_keep.reshape(2, -1, width), grad_came)
    grad_terms = send_column(grad_column)
    out_terms, grad_terms[1], gate_out, up_out, down_out = tie(
        (out_terms, grad_terms[1], gate_out, up_out, down_out)
    )
    layer_out, token_grad = add_all(out_terms), add_all(grad_terms)
    return layer_out, token_grad, gate_out[None], up_out[None], down_out[None]


def solution(mesh):
    in_specs = (
        P(("grp", "exp", "rep"), None),
        P(("grp", "exp", "rep"), None),
        P(("grp", "exp", "rep"), None),
        P(("grp", "exp", "rep"), None),
        P(("grp", "exp"), "rep", None),
        P(("grp", "exp"), "rep", None),
        P(("grp", "exp"), "rep", None),
    )
    out_specs = (
        P(("grp", "exp", "rep"), None),
        P(("grp", "exp", "rep"), None),
        P(("grp", "exp"), "rep", None),
        P(("grp", "exp"), "rep", None),
        P(("grp", "exp"), "rep", None),
    )
    sizes = dict(mesh.shape)
    group_bits = sizes["grp"] & (sizes["grp"] - 1) == 0
    whole_blocks = sizes["exp"] == 4 and sizes["rep"] == 2 and group_bits and sizes["grp"] * sizes["exp"] <= 2 * TOP
    local = dense_local if whole_blocks else routed_local
    return jax.shard_map(local, mesh=mesh, in_specs=in_specs, out_specs=out_specs, check_vma=False)
```

```python
import functools

import jax
import jax.numpy as jnp
from jax import lax
from jax.experimental import pallas as pl
from jax.experimental.pallas import tpu as pltpu
from jax.sharding import PartitionSpec as P

TOP = 8


def partner_2(value, axis, bit):
    mask = 2**bit
    pairs = [(source, source ^ mask) for source in range(lax.axis_size(axis))]
    return lax.ppermute(value, axis, pairs)


def contract_rows(left, right):
    return lax.dot_general(
        left, right, (((0,), (0,)), ((), ())), preferred_element_type=jnp.float32
    )


def contract_cols(left, right):
    return lax.dot_general(
        left, right, (((1,), (1,)), ((), ())), preferred_element_type=jnp.float32
    )


def rounded_sum(first, second):
    left_part = lax.optimization_barrier(first.astype(jnp.bfloat16))
    right_part = lax.optimization_barrier(second.astype(jnp.bfloat16))
    return left_part.astype(jnp.float32) + right_part.astype(jnp.float32)


def routed_local(tokens, cotangent, expert_ids, gate_probs, gate_weight, up_weight, down_weight):
    group_count = lax.axis_size("grp")
    inner_count = lax.axis_size("exp")
    expert_count = group_count * inner_count
    token_count = tokens.shape[0]
    model_width = tokens.shape[1]
    capacity = 3 * token_count * TOP // (2 * expert_count)
    slot_count = expert_count * capacity
    row_count = token_count * TOP
    flat_ids = expert_ids.reshape(row_count)
    flat_probs = gate_probs.reshape(row_count)
    one_hot = (flat_ids[:, None] == jnp.arange(expert_count, dtype=jnp.int32)[None, :]).astype(
        jnp.float32
    )
    earlier = (jnp.arange(row_count)[:, None] > jnp.arange(row_count)[None, :]).astype(jnp.float32)
    counted = jnp.dot(earlier, one_hot, precision=lax.Precision.HIGHEST)
    slot_rank = jnp.sum(counted * one_hot, axis=1).astype(jnp.int32)
    target = flat_ids * capacity + slot_rank
    picked = jnp.arange(slot_count, dtype=jnp.int32)[:, None] == target[None, :]
    slot_probs = jnp.dot(picked.astype(jnp.float32), flat_probs, precision=lax.Precision.HIGHEST)
    pick_tokens = picked.reshape(slot_count, token_count, TOP).any(axis=2).astype(jnp.bfloat16)
    send_tokens = jnp.dot(pick_tokens, tokens, preferred_element_type=jnp.float32).astype(
        jnp.bfloat16
    )
    send_scaled = (
        jnp.dot(pick_tokens, cotangent, preferred_element_type=jnp.float32) * slot_probs[:, None]
    ).astype(jnp.bfloat16)
    whole = (
        lax.all_gather(gate_weight, "rep", axis=1, tiled=True),
        lax.all_gather(up_weight, "rep", axis=1, tiled=True),
        lax.all_gather(down_weight, "rep", axis=1, tiled=True),
    )
    gate_mat = whole[0][0]
    up_mat = whole[1][0]
    down_mat = whole[2][0]
    arrived = (
        lax.all_to_all(
            send_tokens.reshape(expert_count, capacity, model_width),
            ("grp", "exp"),
            split_axis=0,
            concat_axis=0,
            tiled=True,
        ),
        lax.all_to_all(
            send_scaled.reshape(expert_count, capacity, model_width),
            ("grp", "exp"),
            split_axis=0,
            concat_axis=0,
            tiled=True,
        ),
    )
    rows_in = arrived[0].reshape(slot_count, model_width)
    rows_scaled = arrived[1].reshape(slot_count, model_width)
    gate_pre = jnp.dot(rows_in, gate_mat, preferred_element_type=jnp.float32)
    up_pre = jnp.dot(rows_in, up_mat, preferred_element_type=jnp.float32)
    sigma = jax.nn.sigmoid(gate_pre)
    act = gate_pre * sigma
    hidden = (act * up_pre).astype(jnp.bfloat16)
    out_rows = jnp.dot(hidden, down_mat, preferred_element_type=jnp.float32).astype(jnp.bfloat16)
    dhidden = contract_cols(rows_scaled, down_mat)
    dgate = (dhidden * up_pre * sigma * (1.0 + gate_pre * (1.0 - sigma))).astype(jnp.bfloat16)
    dup = (dhidden * act).astype(jnp.bfloat16)
    grad_rows = (contract_cols(dgate, gate_mat) + contract_cols(dup, up_mat)).astype(jnp.bfloat16)
    returned = (
        lax.all_to_all(
            out_rows.reshape(expert_count, capacity, model_width),
            ("grp", "exp"),
            split_axis=0,
            concat_axis=0,
            tiled=True,
        ),
        lax.all_to_all(
            grad_rows.reshape(expert_count, capacity, model_width),
            ("grp", "exp"),
            split_axis=0,
            concat_axis=0,
            tiled=True,
        ),
    )
    replica = lax.axis_index("rep")
    other = 1 - replica
    half_width = gate_weight.shape[1]
    half_hidden = down_weight.shape[1]
    own_in = lax.dynamic_slice_in_dim(rows_in, replica * half_width, half_width, 1)
    own_hidden = lax.dynamic_slice_in_dim(hidden, replica * half_hidden, half_hidden, 1)
    send_in = lax.dynamic_slice_in_dim(rows_in, other * half_width, half_width, 1)
    send_hidden = lax.dynamic_slice_in_dim(hidden, other * half_hidden, half_hidden, 1)
    partner = partner_2((send_in, rows_scaled, send_hidden, dgate, dup), "rep", 0)
    gate_out = rounded_sum(contract_rows(own_in, dgate), contract_rows(partner[0], partner[3]))[
        None
    ]
    up_out = rounded_sum(contract_rows(own_in, dup), contract_rows(partner[0], partner[4]))[None]
    down_out = rounded_sum(
        contract_rows(own_hidden, rows_scaled), contract_rows(partner[2], partner[1])
    )[None]
    back_out = returned[0].reshape(slot_count, model_width)
    back_grad = returned[1].reshape(slot_count, model_width)
    route_out = jnp.dot(picked.T.astype(jnp.bfloat16), back_out, preferred_element_type=jnp.float32)
    layer_out = jnp.sum(
        route_out.reshape(token_count, TOP, model_width) * gate_probs[:, :, None], axis=1
    )
    token_grad = jnp.dot(pick_tokens.T, back_grad, preferred_element_type=jnp.float32)
    return (
        layer_out.astype(jnp.bfloat16),
        token_grad.astype(jnp.bfloat16),
        gate_out.astype(jnp.bfloat16),
        up_out.astype(jnp.bfloat16),
        down_out.astype(jnp.bfloat16),
    )


FIRST, SECOND = (1, 2), (2, 1)
tie = lax.optimization_barrier
VMEM_LIMIT = 56 * 2**20
ANY = pl.BlockSpec(memory_space=pl.ANY)
SMEM = pl.BlockSpec(memory_space=pltpu.SMEM)


def swap_group(value, mask):
    count = lax.axis_size("grp")
    return lax.ppermute(value, "grp", [(i, i ^ mask) for i in range(count)])


def swap_inner(value, masks):
    inner, reps = lax.axis_size("exp"), lax.axis_size("rep")
    pairs = [
        (e * reps + r, (e ^ masks[r]) * reps + r) for e in range(inner) for r in range(reps)
    ]
    return lax.ppermute(value, ("exp", "rep"), pairs)


def steps_of(count):
    steps = [0]
    while len(steps) < count:
        steps = [2 * step for step in steps] + [2 * step + 1 for step in steps]
    return steps


def gather_blocks(block, beside):
    count = lax.axis_size("grp")
    moved, first, second, both = {0: block, 1: swap_group(block, 1)}, {}, {}, {}
    for k in range(count + 1):
        due = [
            (part, step)
            for part, step in ((moved, k), (first, k - 1), (second, k - 1), (both, k - 3))
            if k > 0 and step in part
        ]
        values = beside(k, [part[step] for part, step in due])
        for (part, step), value in zip(due, values):
            part[step] = value
        if k == 0:
            mask = 2
            while mask < count:
                moved[mask] = swap_group(moved[0], mask)
                mask *= 2
        if k < count:
            mask = 1
            while mask < (k & -k):
                moved[k | mask] = swap_group(moved[k], mask)
                mask *= 2
            first[k] = swap_inner(moved[k], FIRST)
            second[k] = swap_group(second[k - 1], 1) if k in (3,) else swap_inner(moved[k], SECOND)
        if k - 1 in ():
            both[k - 1] = swap_group(both[k - 2], 1)
        elif k > 0:
            both[k - 1] = swap_inner(first[k - 1], SECOND)
    return [part[step] for part in (moved, first, second, both) for step in steps_of(count)]


def add_bf16(left, right):
    return (left.astype(jnp.float32) + right.astype(jnp.float32)).astype(jnp.bfloat16)


def reduce_part(here, came):
    came = came.reshape(here.shape)
    passed = swap_inner(add_bf16(here[1], came[1]), FIRST)
    return add_bf16(here[0].astype(jnp.float32) + came[0].astype(jnp.float32), passed)


def send_column(column):
    count = lax.axis_size("grp")
    rows = column.shape[0] // count
    return [
        column[q * rows : (q + 1) * rows] if step == 0
        else swap_group(column[q * rows : (q + 1) * rows], step)
        for q, step in enumerate(steps_of(count))
    ]


def halve_column(column, masks):
    for mask in masks:
        half = column.shape[0] // 2
        column = add_bf16(column[:half], swap_group(column[half:], mask))
    return column


def add_all(values):
    total = values[0].astype(jnp.float32)
    for value in values[1:]:
        total = total + value.astype(jnp.float32)
    return total.astype(jnp.bfloat16)


def token_block(tokens, cotangent, expert_ids, gate_probs, expert_count):
    named = expert_ids[:, :, None] == jnp.arange(expert_count, dtype=jnp.int32)
    rest = jnp.sum(jnp.where(named, gate_probs[:, :, None], 0.0), axis=1)
    terms = []
    for _ in range(3):
        terms.append(lax.reduce_precision(rest, exponent_bits=8, mantissa_bits=7))
        rest = rest - terms[-1]
    terms = jnp.concatenate(terms, axis=1).astype(jnp.bfloat16)
    rows, side = tokens.shape[0], side_width(expert_count)
    terms = jnp.pad(terms, ((0, rows), (0, side - terms.shape[1])))
    return jnp.concatenate([jnp.concatenate([tokens, cotangent], axis=0), terms], axis=1)


def side_width(expert_count):
    return -(-3 * expert_count // 128) * 128


def start_halves(halves, whole, sems, first_sem, replica):
    own, partner = halves
    size = own.shape[0]
    copies = []
    for k, (half, which) in enumerate(((own, replica), (partner, 1 - replica))):
        place = pl.ds(pl.multiple_of(which * size, size), size)
        copies.append(pltpu.make_async_copy(half, whole.at[place, :], sems.at[first_sem + k]))
        copies[-1].start()
    return copies


def start_rows(pieces, whole, offset, rows, first_col, sems):
    copies = []
    for k, piece in enumerate(pieces):
        part = piece.at[pl.ds(offset, rows), pl.ds(first_col, whole.shape[1])]
        copies.append(pltpu.make_async_copy(part, whole.at[pl.ds(k * rows, rows), :], sems.at[k]))
        copies[-1].start()
    return copies


def start_out(sources_and_places, sems, first_sem):
    copies = []
    for k, (source, place) in enumerate(sources_and_places):
        copies.append(pltpu.make_async_copy(source, place, sems.at[first_sem + k]))
        copies[-1].start()
    return copies


def start_parts(parts, whole, sems, first_sem):
    size = parts[0].shape[0]
    places = [whole.at[pl.ds(k * size, size), :] for k in range(len(parts))]
    return start_out(list(zip(parts, places)), sems, first_sem)


def wait_all(copies):
    for copy in copies:
        copy.wait()


def weights_of(side_ref, expert, expert_count):
    lane = lax.broadcasted_iota(jnp.int32, side_ref.shape, 1)
    mine = (lane == expert) | (lane == expert + expert_count) | (lane == expert + 2 * expert_count)
    return jnp.sum(jnp.where(mine, side_ref[...].astype(jnp.float32), 0.0), axis=1, keepdims=True)


def halves_of(whole, cols, keep, send):
    half = keep.shape[0]
    return [
        (whole.at[pl.ds(0, half), cols], keep.at[:, cols]),
        (whole.at[pl.ds(half, half), cols], send.at[:, cols]),
    ]


def tiles(size, count):
    return [pl.ds(i * size // count, size // count) for i in range(count)]


def assemble_kernel(rows, count, *refs):
    pieces, halves, refs = refs[:count], refs[count : count + 2], refs[count + 2 :]
    whole_out, hidden_out, whole, hidden, sems, half_sems, out_sems = refs
    copies = start_rows(pieces, whole, 0, rows, 0, sems)
    wait_all(copies + start_parts(halves, hidden, half_sems, 0))
    wait_all(start_out([(whole, whole_out), (hidden, hidden_out)], out_sems, 0))


def forward_kernel(rows, count, expert_count, where_ref, *refs):
    pieces, refs = refs[:count], refs[count:]
    gate, up, down = refs[0:2], refs[2:4], refs[4:6]
    whole_out, gate_pre_out, up_pre_out, hidden_out = refs[6:10]
    rows_in, side, gate_all, up_all, down_all, gate_pre, up_pre, hidden, out = refs[10:19]
    row_sems, side_sems, weight_sems, out_sems = refs[19:]
    width = rows_in.shape[1]
    row_copies = start_rows(pieces, rows_in, 0, rows, 0, row_sems)
    gate_copies = start_halves(gate, gate_all, weight_sems, 0, where_ref[0])
    wait_all(row_copies)
    up_copies = start_halves(up, up_all, weight_sems, 2, where_ref[0])
    wait_all(gate_copies)
    side_copies = start_rows(pieces, side, 0, rows, width, side_sems)
    down_copies = start_halves(down, down_all, weight_sems, 4, where_ref[0])
    pre = jnp.dot(rows_in[...], gate_all[...], preferred_element_type=jnp.float32)
    gate_pre[...] = pre.astype(gate_pre.dtype)
    act = pre * jax.nn.sigmoid(pre)
    wait_all(up_copies)
    pre = jnp.dot(rows_in[...], up_all[...], preferred_element_type=jnp.float32)
    up_pre[...] = pre.astype(up_pre.dtype)
    hidden[...] = (act * pre).astype(jnp.bfloat16)
    outs = start_out(
        [(gate_pre, gate_pre_out), (up_pre, up_pre_out), (hidden, hidden_out)], out_sems, 0
    )
    wait_all(side_copies)
    probs = weights_of(side, where_ref[1], expert_count)
    wait_all(down_copies)
    for t, cols in enumerate(tiles(width, 2)):
        part = jnp.dot(hidden[...], down_all[:, cols], preferred_element_type=jnp.float32)
        out[:, cols] = (part * probs).astype(jnp.bfloat16)
        outs += start_out([(out.at[:, cols], whole_out.at[:, cols])], out_sems, 3 + t)
    wait_all(outs)


def backward_kernel(rows, count, where_ref, *refs):
    gate_pre_in, up_pre_in, refs = refs[0:2], refs[2:4], refs[4:]
    pieces, refs = refs[:count], refs[count:]
    gate, up, down = refs[0:2], refs[2:4], refs[4:6]
    keep, send, dgate_out, dup_out, scaled_out = refs[6:11]
    scaled, side, gate_all, up_all, down_all, gate_pre, up_pre, dgate, dup, grad = refs[11:21]
    row_sems, side_sems, weight_sems, pre_sems, out_sems = refs[21:]
    width = scaled.shape[1]
    row_copies = start_rows(pieces, scaled, rows, rows, 0, row_sems)
    side_copies = start_rows(pieces, side, 0, rows, width, side_sems)
    down_copies = start_halves(down, down_all, weight_sems, 4, where_ref[0])
    pre_copies = start_parts(gate_pre_in, gate_pre, pre_sems, 0)
    pre_copies += start_parts(up_pre_in, up_pre, pre_sems, 2)
    wait_all(row_copies + side_copies)
    gate_copies = start_halves(gate, gate_all, weight_sems, 0, where_ref[0])
    up_copies = start_halves(up, up_all, weight_sems, 2, where_ref[0])
    probs = weights_of(side, where_ref[1], count)
    scaled[...] = (scaled[...].astype(jnp.float32) * probs).astype(jnp.bfloat16)
    outs = start_out([(scaled, scaled_out)], out_sems, 0)
    wait_all(down_copies)
    dhidden = contract_cols(scaled[...], down_all[...])
    wait_all(pre_copies)
    pre, gain = gate_pre[...].astype(jnp.float32), up_pre[...].astype(jnp.float32)
    sigma = jax.nn.sigmoid(pre)
    dgate[...] = (dhidden * gain * sigma * (1.0 + pre * (1.0 - sigma))).astype(jnp.bfloat16)
    dup[...] = (dhidden * (pre * sigma)).astype(jnp.bfloat16)
    outs += start_out([(dgate, dgate_out), (dup, dup_out)], out_sems, 1)
    wait_all(gate_copies + up_copies)
    for t, cols in enumerate(tiles(width, 2)):
        part = contract_cols(dgate[...], gate_all[cols, :])
        grad[:, cols] = (part + contract_cols(dup[...], up_all[cols, :])).astype(jnp.bfloat16)
        outs += start_out(halves_of(grad, cols, keep, send), out_sems, 3 + 2 * t)
    wait_all(outs)


def expert_call(kernel, outs, scratch, sems, flops, inputs):
    return pl.pallas_call(
        kernel,
        out_shape=[jax.ShapeDtypeStruct(shape, dtype) for shape, dtype in outs],
        in_specs=[SMEM] + [ANY] * (len(inputs) - 1),
        out_specs=[ANY] * len(outs),
        scratch_shapes=[pltpu.VMEM(shape, dtype) for shape, dtype in scratch]
        + [pltpu.SemaphoreType.DMA((n,)) for n in sems],
        compiler_params=pltpu.CompilerParams(vmem_limit_bytes=VMEM_LIMIT),
        cost_estimate=pl.CostEstimate(
            flops=flops,
            bytes_accessed=sum(2 * value.size for value in inputs),
            transcendentals=0,
        ),
    )(*inputs)


class PartnerWeights:
    def __init__(self, own):
        self.own, self.came = list(own), []

    def __call__(self, step, values):
        if not values:
            return values
        k = len(self.came)
        old, new = self.came[k - 1 :] if k > 1 else [], self.own[k : k + 1]
        values = list(tie((*values, *old, *new)))
        if new:
            self.came.append(partner_2(values.pop(), "rep", 0))
        if old:
            self.came[k - 1] = values.pop()
        return values


def dense_local(tokens, cotangent, expert_ids, gate_probs, gate_weight, up_weight, down_weight):
    expert_count = lax.axis_size("grp") * lax.axis_size("exp")
    replica = lax.axis_index("rep")
    rows, width = tokens.shape
    half_width, hidden_width = gate_weight.shape[1:]
    half_hidden = down_weight.shape[1]
    total = expert_count * rows
    own = (gate_weight[0], up_weight[0], down_weight[0])
    partner = PartnerWeights(own)
    block = token_block(tokens, cotangent, expert_ids, gate_probs, expert_count)
    pieces = gather_blocks(block, partner)
    partner = partner.came
    weights = [value for pair in zip(own, partner) for value in pair]
    expert = lax.axis_index("grp") * lax.axis_size("exp") + lax.axis_index("exp")
    where = jnp.stack([replica, expert]).astype(jnp.int32)
    bf16 = jnp.bfloat16
    wide, narrow = ((total, width), bf16), ((total, hidden_width), bf16)
    half_wide = ((total // 2, width), bf16)
    half_narrow = ((total // 2, hidden_width), bf16)
    mats = [
        ((width, hidden_width), bf16),
        ((width, hidden_width), bf16),
        ((hidden_width, width), bf16),
    ]
    side = side_width(expert_count)
    flops = 6 * total * width * hidden_width
    half_count = expert_count // 2
    forward, waiting = [], pieces[half_count:]
    for half_pieces in (pieces[:half_count], None):
        forward.append(
            list(expert_call(
                functools.partial(forward_kernel, rows, half_count, expert_count),
                [half_wide] + [half_narrow] * 3,
                [half_wide, ((total // 2, side), bf16), *mats] + [half_narrow] * 3 + [half_wide],
                [half_count, half_count, 6, 5],
                flops // 2,
                [where, *(half_pieces or waiting), *weights],
            ))
        )
        if half_pieces:
            forward[0][0], waiting = tie((forward[0][0], waiting))
    (out_keep, out_send), gate_pre, up_pre, hidden = zip(*forward)
    held = [wide, ((total, side), bf16), *mats, narrow, narrow]
    out_came = swap_inner(out_send, SECOND)
    rows_in, hidden = pl.pallas_call(
        functools.partial(assemble_kernel, rows, expert_count),
        out_shape=[jax.ShapeDtypeStruct(*wide), jax.ShapeDtypeStruct(*narrow)],
        in_specs=[ANY] * (expert_count + 2),
        out_specs=[ANY, ANY],
        scratch_shapes=[
            pltpu.VMEM(*wide),
            pltpu.VMEM(*narrow),
            pltpu.SemaphoreType.DMA((expert_count,)),
            pltpu.SemaphoreType.DMA((2,)),
            pltpu.SemaphoreType.DMA((2,)),
        ],
        compiler_params=pltpu.CompilerParams(vmem_limit_bytes=VMEM_LIMIT // 4),
    )(*pieces, *hidden)
    grad_keep, grad_send, dgate, dup, rows_scaled = expert_call(
        functools.partial(backward_kernel, rows, expert_count),
        [half_wide, half_wide, narrow, narrow, wide],
        held + [narrow, narrow, wide],
        [expert_count, expert_count, 6, 4, 7],
        flops,
        [where, *gate_pre, *up_pre, *pieces, *weights],
    )
    out_came, grad_keep, grad_send, dgate, dup, rows_scaled = tie(
        (out_came, grad_keep, grad_send, dgate, dup, rows_scaled)
    )
    grad_came = swap_inner(grad_send, SECOND)
    out_column = reduce_part(out_keep.reshape(2, -1, width), out_came)
    grad_came, out_column, dgate, dup, rows_scaled, hidden, rows_in = tie(
        (grad_came, out_column, dgate, dup, rows_scaled, hidden, rows_in)
    )

    def half(value, which, size):
        return lax.dynamic_slice_in_dim(value, which * size, size, 1)

    other = 1 - replica
    sent = (
        contract_rows(half(rows_in, other, half_width), dgate).astype(bf16),
        contract_rows(half(rows_in, other, half_width), dup).astype(bf16),
        contract_rows(half(hidden, other, half_hidden), rows_scaled).astype(bf16),
    )
    back = partner_2(sent, "rep", 0)
    gate_out = add_bf16(contract_rows(half(rows_in, replica, half_width), dgate), back[0])
    up_out = add_bf16(contract_rows(half(rows_in, replica, half_width), dup), back[1])
    down_out = add_bf16(contract_rows(half(hidden, replica, half_hidden), rows_scaled), back[2])
    masks = [2**bit for bit in range(lax.axis_size("grp").bit_length() - 1)]
    out_column = halve_column(out_column, masks[:-1])
    half = out_column.shape[0] // 2
    out_terms = [out_column[:half], swap_group(out_column[half:], masks[-1])]
    grad_column = reduce_part(grad_keep.reshape(2, -1, width), grad_came)
    grad_terms = send_column(grad_column)
    out_terms, grad_terms[1], gate_out, up_out, down_out = tie(
        (out_terms, grad_terms[1], gate_out, up_out, down_out)
    )
    layer_out, token_grad = add_all(out_terms), add_all(grad_terms)
    return layer_out, token_grad, gate_out[None], up_out[None], down_out[None]


def solution(mesh):
    in_specs = (
        P(("grp", "exp", "rep"), None),
        P(("grp", "exp", "rep"), None),
        P(("grp", "exp", "rep"), None),
        P(("grp", "exp", "rep"), None),
        P(("grp", "exp"), "rep", None),
        P(("grp", "exp"), "rep", None),
        P(("grp", "exp"), "rep", None),
    )
    out_specs = (
        P(("grp", "exp", "rep"), None),
        P(("grp", "exp", "rep"), None),
        P(("grp", "exp"), "rep", None),
        P(("grp", "exp"), "rep", None),
        P(("grp", "exp"), "rep", None),
    )
    sizes = dict(mesh.shape)
    group_bits = sizes["grp"] & (sizes["grp"] - 1) == 0
    whole_blocks = sizes["exp"] == 4 and sizes["rep"] == 2 and group_bits and sizes["grp"] * sizes["exp"] <= 2 * TOP
    local = dense_local if whole_blocks else routed_local
    return jax.shard_map(local, mesh=mesh, in_specs=in_specs, out_specs=out_specs, check_vma=False)
```

```python
import functools

import jax
import jax.numpy as jnp
from jax import lax
from jax.experimental import pallas as pl
from jax.experimental.pallas import tpu as pltpu
from jax.sharding import PartitionSpec as P

TOP = 8


def partner_2(value, axis, bit):
    mask = 2**bit
    pairs = [(source, source ^ mask) for source in range(lax.axis_size(axis))]
    return lax.ppermute(value, axis, pairs)


def contract_rows(left, right):
    return lax.dot_general(
        left, right, (((0,), (0,)), ((), ())), preferred_element_type=jnp.float32
    )


def contract_cols(left, right):
    return lax.dot_general(
        left, right, (((1,), (1,)), ((), ())), preferred_element_type=jnp.float32
    )


def rounded_sum(first, second):
    left_part = lax.optimization_barrier(first.astype(jnp.bfloat16))
    right_part = lax.optimization_barrier(second.astype(jnp.bfloat16))
    return left_part.astype(jnp.float32) + right_part.astype(jnp.float32)


def routed_local(tokens, cotangent, expert_ids, gate_probs, gate_weight, up_weight, down_weight):
    group_count = lax.axis_size("grp")
    inner_count = lax.axis_size("exp")
    expert_count = group_count * inner_count
    token_count = tokens.shape[0]
    model_width = tokens.shape[1]
    capacity = 3 * token_count * TOP // (2 * expert_count)
    slot_count = expert_count * capacity
    row_count = token_count * TOP
    flat_ids = expert_ids.reshape(row_count)
    flat_probs = gate_probs.reshape(row_count)
    one_hot = (flat_ids[:, None] == jnp.arange(expert_count, dtype=jnp.int32)[None, :]).astype(
        jnp.float32
    )
    earlier = (jnp.arange(row_count)[:, None] > jnp.arange(row_count)[None, :]).astype(jnp.float32)
    counted = jnp.dot(earlier, one_hot, precision=lax.Precision.HIGHEST)
    slot_rank = jnp.sum(counted * one_hot, axis=1).astype(jnp.int32)
    target = flat_ids * capacity + slot_rank
    picked = jnp.arange(slot_count, dtype=jnp.int32)[:, None] == target[None, :]
    slot_probs = jnp.dot(picked.astype(jnp.float32), flat_probs, precision=lax.Precision.HIGHEST)
    pick_tokens = picked.reshape(slot_count, token_count, TOP).any(axis=2).astype(jnp.bfloat16)
    send_tokens = jnp.dot(pick_tokens, tokens, preferred_element_type=jnp.float32).astype(
        jnp.bfloat16
    )
    send_scaled = (
        jnp.dot(pick_tokens, cotangent, preferred_element_type=jnp.float32) * slot_probs[:, None]
    ).astype(jnp.bfloat16)
    whole = (
        lax.all_gather(gate_weight, "rep", axis=1, tiled=True),
        lax.all_gather(up_weight, "rep", axis=1, tiled=True),
        lax.all_gather(down_weight, "rep", axis=1, tiled=True),
    )
    gate_mat = whole[0][0]
    up_mat = whole[1][0]
    down_mat = whole[2][0]
    arrived = (
        lax.all_to_all(
            send_tokens.reshape(expert_count, capacity, model_width),
            ("grp", "exp"),
            split_axis=0,
            concat_axis=0,
            tiled=True,
        ),
        lax.all_to_all(
            send_scaled.reshape(expert_count, capacity, model_width),
            ("grp", "exp"),
            split_axis=0,
            concat_axis=0,
            tiled=True,
        ),
    )
    rows_in = arrived[0].reshape(slot_count, model_width)
    rows_scaled = arrived[1].reshape(slot_count, model_width)
    gate_pre = jnp.dot(rows_in, gate_mat, preferred_element_type=jnp.float32)
    up_pre = jnp.dot(rows_in, up_mat, preferred_element_type=jnp.float32)
    sigma = jax.nn.sigmoid(gate_pre)
    act = gate_pre * sigma
    hidden = (act * up_pre).astype(jnp.bfloat16)
    out_rows = jnp.dot(hidden, down_mat, preferred_element_type=jnp.float32).astype(jnp.bfloat16)
    dhidden = contract_cols(rows_scaled, down_mat)
    dgate = (dhidden * up_pre * sigma * (1.0 + gate_pre * (1.0 - sigma))).astype(jnp.bfloat16)
    dup = (dhidden * act).astype(jnp.bfloat16)
    grad_rows = (contract_cols(dgate, gate_mat) + contract_cols(dup, up_mat)).astype(jnp.bfloat16)
    returned = (
        lax.all_to_all(
            out_rows.reshape(expert_count, capacity, model_width),
            ("grp", "exp"),
            split_axis=0,
            concat_axis=0,
            tiled=True,
        ),
        lax.all_to_all(
            grad_rows.reshape(expert_count, capacity, model_width),
            ("grp", "exp"),
            split_axis=0,
            concat_axis=0,
            tiled=True,
        ),
    )
    replica = lax.axis_index("rep")
    other = 1 - replica
    half_width = gate_weight.shape[1]
    half_hidden = down_weight.shape[1]
    own_in = lax.dynamic_slice_in_dim(rows_in, replica * half_width, half_width, 1)
    own_hidden = lax.dynamic_slice_in_dim(hidden, replica * half_hidden, half_hidden, 1)
    send_in = lax.dynamic_slice_in_dim(rows_in, other * half_width, half_width, 1)
    send_hidden = lax.dynamic_slice_in_dim(hidden, other * half_hidden, half_hidden, 1)
    partner = partner_2((send_in, rows_scaled, send_hidden, dgate, dup), "rep", 0)
    gate_out = rounded_sum(contract_rows(own_in, dgate), contract_rows(partner[0], partner[3]))[
        None
    ]
    up_out = rounded_sum(contract_rows(own_in, dup), contract_rows(partner[0], partner[4]))[None]
    down_out = rounded_sum(
        contract_rows(own_hidden, rows_scaled), contract_rows(partner[2], partner[1])
    )[None]
    back_out = returned[0].reshape(slot_count, model_width)
    back_grad = returned[1].reshape(slot_count, model_width)
    route_out = jnp.dot(picked.T.astype(jnp.bfloat16), back_out, preferred_element_type=jnp.float32)
    layer_out = jnp.sum(
        route_out.reshape(token_count, TOP, model_width) * gate_probs[:, :, None], axis=1
    )
    token_grad = jnp.dot(pick_tokens.T, back_grad, preferred_element_type=jnp.float32)
    return (
        layer_out.astype(jnp.bfloat16),
        token_grad.astype(jnp.bfloat16),
        gate_out.astype(jnp.bfloat16),
        up_out.astype(jnp.bfloat16),
        down_out.astype(jnp.bfloat16),
    )


FIRST, SECOND = (1, 2), (2, 1)
tie = lax.optimization_barrier
VMEM_LIMIT = 32 * 2**20
ANY = pl.BlockSpec(memory_space=pl.ANY)
VMEM = pl.BlockSpec(memory_space=pltpu.VMEM)
SMEM = pl.BlockSpec(memory_space=pltpu.SMEM)


def swap_group(value, mask):
    count = lax.axis_size("grp")
    return lax.ppermute(value, "grp", [(i, i ^ mask) for i in range(count)])


def swap_inner(value, masks):
    inner, reps = lax.axis_size("exp"), lax.axis_size("rep")
    pairs = [
        (e * reps + r, (e ^ masks[r]) * reps + r) for e in range(inner) for r in range(reps)
    ]
    return lax.ppermute(value, ("exp", "rep"), pairs)


def steps_of(count):
    steps = [0]
    while len(steps) < count:
        steps = [2 * step for step in steps] + [2 * step + 1 for step in steps]
    return steps


def gather_blocks(block, beside):
    count = lax.axis_size("grp")
    moved, first, second, both = {0: block, 1: swap_group(block, 1)}, {}, {}, {}
    for k in range(count + 1):
        due = [
            (part, step)
            for part, step in ((moved, k), (first, k - 1), (second, k - 1), (both, k - 3))
            if k > 0 and step in part
        ]
        values = beside(k, [part[step] for part, step in due])
        for (part, step), value in zip(due, values):
            part[step] = value
        if k == 0:
            mask = 2
            while mask < count:
                moved[mask] = swap_group(moved[0], mask)
                mask *= 2
        if k < count:
            mask = 1
            while mask < (k & -k):
                moved[k | mask] = swap_group(moved[k], mask)
                mask *= 2
            first[k] = swap_inner(moved[k], FIRST)
            second[k] = swap_group(second[k - 1], 1) if k in (3,) else swap_inner(moved[k], SECOND)
        if k - 1 in ():
            both[k - 1] = swap_group(both[k - 2], 1)
        elif k > 0:
            both[k - 1] = swap_inner(first[k - 1], SECOND)
    return [part[step] for part in (moved, first, second, both) for step in steps_of(count)]


def add_bf16(left, right):
    return (left.astype(jnp.float32) + right.astype(jnp.float32)).astype(jnp.bfloat16)


def reduce_part(here, came):
    came = came.reshape(here.shape)
    passed = swap_inner(add_bf16(here[1], came[1]), FIRST)
    return add_bf16(here[0].astype(jnp.float32) + came[0].astype(jnp.float32), passed)


def send_column(column):
    count = lax.axis_size("grp")
    rows = column.shape[0] // count
    return [
        column[q * rows : (q + 1) * rows] if step == 0
        else swap_group(column[q * rows : (q + 1) * rows], step)
        for q, step in enumerate(steps_of(count))
    ]


def halve_column(column, masks):
    for mask in masks:
        half = column.shape[0] // 2
        column = add_bf16(column[:half], swap_group(column[half:], mask))
    return column


def add_all(values):
    total = values[0].astype(jnp.float32)
    for value in values[1:]:
        total = total + value.astype(jnp.float32)
    return total.astype(jnp.bfloat16)


def token_block(tokens, cotangent, expert_ids, gate_probs, expert_count):
    named = expert_ids[:, :, None] == jnp.arange(expert_count, dtype=jnp.int32)
    rest = jnp.sum(jnp.where(named, gate_probs[:, :, None], 0.0), axis=1)
    terms = []
    for _ in range(3):
        terms.append(lax.reduce_precision(rest, exponent_bits=8, mantissa_bits=7))
        rest = rest - terms[-1]
    terms = jnp.concatenate(terms, axis=1).astype(jnp.bfloat16)
    rows, side = tokens.shape[0], side_width(expert_count)
    terms = jnp.pad(terms, ((0, rows), (0, side - terms.shape[1])))
    return jnp.concatenate([jnp.concatenate([tokens, cotangent], axis=0), terms], axis=1)


def side_width(expert_count):
    return -(-3 * expert_count // 128) * 128


def start_halves(halves, whole, sems, first_sem, replica):
    own, partner = halves
    size = own.shape[0]
    copies = []
    for k, (half, which) in enumerate(((own, replica), (partner, 1 - replica))):
        place = pl.ds(pl.multiple_of(which * size, size), size)
        copies.append(pltpu.make_async_copy(half, whole.at[place, :], sems.at[first_sem + k]))
        copies[-1].start()
    return copies


def start_rows(pieces, whole, offset, rows, first_col, sems):
    copies = []
    for k, piece in enumerate(pieces):
        part = piece.at[pl.ds(offset, rows), pl.ds(first_col, whole.shape[1])]
        copies.append(pltpu.make_async_copy(part, whole.at[pl.ds(k * rows, rows), :], sems.at[k]))
        copies[-1].start()
    return copies


def start_out(sources_and_places, sems, first_sem):
    copies = []
    for k, (source, place) in enumerate(sources_and_places):
        copies.append(pltpu.make_async_copy(source, place, sems.at[first_sem + k]))
        copies[-1].start()
    return copies


def start_parts(parts, whole, sems, first_sem):
    size = parts[0].shape[0]
    places = [whole.at[pl.ds(k * size, size), :] for k in range(len(parts))]
    return start_out(list(zip(parts, places)), sems, first_sem)


def wait_all(copies):
    for copy in copies:
        copy.wait()


def weights_of(side_ref, expert, expert_count):
    lane = lax.broadcasted_iota(jnp.int32, side_ref.shape, 1)
    mine = (lane == expert) | (lane == expert + expert_count) | (lane == expert + 2 * expert_count)
    return jnp.sum(jnp.where(mine, side_ref[...].astype(jnp.float32), 0.0), axis=1, keepdims=True)


def halves_of(whole, cols, keep, send):
    half = keep.shape[0]
    return [
        (whole.at[pl.ds(0, half), cols], keep.at[:, cols]),
        (whole.at[pl.ds(half, half), cols], send.at[:, cols]),
    ]


def tiles(size, count):
    return [pl.ds(i * size // count, size // count) for i in range(count)]


def assemble_kernel(rows, count, *refs):
    pieces, halves, refs = refs[:count], refs[count : count + 2], refs[count + 2 :]
    whole_out, hidden_out, whole, hidden, sems, half_sems, out_sems = refs
    copies = start_rows(pieces, whole, 0, rows, 0, sems)
    wait_all(copies + start_parts(halves, hidden, half_sems, 0))
    wait_all(start_out([(whole, whole_out), (hidden, hidden_out)], out_sems, 0))


def weights_kernel(where_ref, *refs):
    wholes, where_out, sems = refs[6:9], refs[9], refs[10]
    copies = []
    for k, whole in enumerate(wholes):
        copies += start_halves(refs[2 * k : 2 * k + 2], whole, sems, 2 * k, where_ref[0])
    for k in range(where_out.shape[0]):
        where_out[k] = where_ref[k]
    wait_all(copies)


def forward_kernel(rows, count, expert_count, where_ref, *refs):
    pieces, refs = refs[:count], refs[count:]
    gate_all, up_all, down_all = refs[0:3]
    whole_out, gate_pre_out, up_pre_out, hidden_out = refs[3:7]
    rows_in, side, gate_pre, up_pre, hidden, out = refs[7:13]
    row_sems, side_sems, out_sems = refs[13:]
    width = rows_in.shape[1]
    row_copies = start_rows(pieces, rows_in, 0, rows, 0, row_sems)
    side_copies = start_rows(pieces, side, 0, rows, width, side_sems)
    wait_all(row_copies)
    pre = jnp.dot(rows_in[...], gate_all[...], preferred_element_type=jnp.float32)
    gate_pre[...] = pre.astype(gate_pre.dtype)
    act = pre * jax.nn.sigmoid(pre)
    pre = jnp.dot(rows_in[...], up_all[...], preferred_element_type=jnp.float32)
    up_pre[...] = pre.astype(up_pre.dtype)
    hidden[...] = (act * pre).astype(jnp.bfloat16)
    outs = start_out(
        [(gate_pre, gate_pre_out), (up_pre, up_pre_out), (hidden, hidden_out)], out_sems, 0
    )
    wait_all(side_copies)
    probs = weights_of(side, where_ref[1], expert_count)
    for t, cols in enumerate(tiles(width, 2)):
        part = jnp.dot(hidden[...], down_all[:, cols], preferred_element_type=jnp.float32)
        out[:, cols] = (part * probs).astype(jnp.bfloat16)
        outs += start_out([(out.at[:, cols], whole_out.at[:, cols])], out_sems, 3 + t)
    wait_all(outs)


def backward_kernel(rows, count, where_ref, *refs):
    gate_pre_in, up_pre_in, refs = refs[0:2], refs[2:4], refs[4:]
    pieces, refs = refs[:count], refs[count:]
    gate_all, up_all, down_all = refs[0:3]
    keep, send, dgate_out, dup_out, scaled_out = refs[3:8]
    scaled, side, gate_pre, up_pre, dgate, dup, grad = refs[8:15]
    row_sems, side_sems, pre_sems, out_sems = refs[15:]
    width = scaled.shape[1]
    row_copies = start_rows(pieces, scaled, rows, rows, 0, row_sems)
    side_copies = start_rows(pieces, side, 0, rows, width, side_sems)
    pre_copies = start_parts(gate_pre_in, gate_pre, pre_sems, 0)
    pre_copies += start_parts(up_pre_in, up_pre, pre_sems, 2)
    wait_all(row_copies + side_copies)
    probs = weights_of(side, where_ref[1], count)
    scaled[...] = (scaled[...].astype(jnp.float32) * probs).astype(jnp.bfloat16)
    outs = start_out([(scaled, scaled_out)], out_sems, 0)
    dhidden = contract_cols(scaled[...], down_all[...])
    wait_all(pre_copies)
    pre, gain = gate_pre[...].astype(jnp.float32), up_pre[...].astype(jnp.float32)
    sigma = jax.nn.sigmoid(pre)
    dgate[...] = (dhidden * gain * sigma * (1.0 + pre * (1.0 - sigma))).astype(jnp.bfloat16)
    dup[...] = (dhidden * (pre * sigma)).astype(jnp.bfloat16)
    outs += start_out([(dgate, dgate_out), (dup, dup_out)], out_sems, 1)
    for t, cols in enumerate(tiles(width, 2)):
        part = contract_cols(dgate[...], gate_all[cols, :])
        grad[:, cols] = (part + contract_cols(dup[...], up_all[cols, :])).astype(jnp.bfloat16)
        outs += start_out(halves_of(grad, cols, keep, send), out_sems, 3 + 2 * t)
    wait_all(outs)


def in_hbm(values):
    return [pltpu.with_memory_space_constraint(value, pltpu.HBM) for value in values]


def expert_call(kernel, outs, scratch, sems, flops, inputs):
    return pl.pallas_call(
        kernel,
        out_shape=[pltpu.HBM(shape, dtype) for shape, dtype in outs],
        in_specs=[SMEM] + [ANY] * (len(inputs) - 4) + [VMEM] * 3,
        out_specs=[ANY] * len(outs),
        scratch_shapes=[pltpu.VMEM(shape, dtype) for shape, dtype in scratch]
        + [pltpu.SemaphoreType.DMA((n,)) for n in sems],
        compiler_params=pltpu.CompilerParams(vmem_limit_bytes=VMEM_LIMIT),
        cost_estimate=pl.CostEstimate(
            flops=flops,
            bytes_accessed=sum(2 * value.size for value in inputs),
            transcendentals=0,
        ),
    )(inputs[0], *in_hbm(inputs[1:-3]), *inputs[-3:])


class WholeWeights:
    def __init__(self, own, where):
        self.own, self.where, self.came, self.whole = list(own), where, [], None

    def load(self):
        width, hidden_width = 2 * self.own[0].shape[0], self.own[0].shape[1]
        shapes = [(width, hidden_width), (width, hidden_width), (hidden_width, width)]
        halves = [value for pair in zip(self.own, self.came) for value in pair]
        *self.whole, self.where = pl.pallas_call(
            weights_kernel,
            out_shape=[pltpu.VMEM(shape, jnp.bfloat16) for shape in shapes]
            + [jax.ShapeDtypeStruct(self.where.shape, self.where.dtype)],
            in_specs=[SMEM] + [ANY] * 6,
            out_specs=[VMEM] * 3 + [SMEM],
            scratch_shapes=[pltpu.SemaphoreType.DMA((6,))],
            compiler_params=pltpu.CompilerParams(vmem_limit_bytes=VMEM_LIMIT),
        )(self.where, *in_hbm(halves))
        self.whole = [pltpu.with_memory_space_constraint(w, pltpu.VMEM) for w in self.whole]

    def __call__(self, step, values):
        if not values:
            return values
        count = len(values)
        if step <= 2:
            new = self.own[:1] if step == 1 else self.own[1:]
            values = list(tie((*values, *new)))
            self.came += [partner_2(value, "rep", 0) for value in values[count:]]
        elif self.whole is None:
            self.load()
            *values, self.where = tie((*values, self.where))
        return values[:count]


def dense_local(tokens, cotangent, expert_ids, gate_probs, gate_weight, up_weight, down_weight):
    expert_count = lax.axis_size("grp") * lax.axis_size("exp")
    replica = lax.axis_index("rep")
    rows, width = tokens.shape
    half_width, hidden_width = gate_weight.shape[1:]
    half_hidden = down_weight.shape[1]
    total = expert_count * rows
    own = (gate_weight[0], up_weight[0], down_weight[0])
    expert = lax.axis_index("grp") * lax.axis_size("exp") + lax.axis_index("exp")
    where = jnp.stack([replica, expert]).astype(jnp.int32)
    block = token_block(tokens, cotangent, expert_ids, gate_probs, expert_count)
    collected = WholeWeights(own, where)
    pieces = gather_blocks(block, collected)
    if collected.whole is None:
        collected.load()
    weights, where = collected.whole, collected.where
    bf16 = jnp.bfloat16
    wide, narrow = ((total, width), bf16), ((total, hidden_width), bf16)
    half_wide = ((total // 2, width), bf16)
    half_narrow = ((total // 2, hidden_width), bf16)
    side = side_width(expert_count)
    flops = 6 * total * width * hidden_width
    half_count = expert_count // 2
    forward, waiting = [], pieces[half_count:]
    for half_pieces in (pieces[:half_count], None):
        forward.append(
            list(expert_call(
                functools.partial(forward_kernel, rows, half_count, expert_count),
                [half_wide] + [half_narrow] * 3,
                [half_wide, ((total // 2, side), bf16)] + [half_narrow] * 3 + [half_wide],
                [half_count, half_count, 5],
                flops // 2,
                [where, *(half_pieces or waiting), *weights],
            ))
        )
        if half_pieces:
            forward[0][0], waiting = tie((forward[0][0], waiting))
    (out_keep, out_send), gate_pre, up_pre, hidden = zip(*forward)
    held = [wide, ((total, side), bf16), narrow, narrow]
    out_came = swap_inner(out_send, SECOND)
    rows_in, hidden = pl.pallas_call(
        functools.partial(assemble_kernel, rows, expert_count),
        out_shape=[jax.ShapeDtypeStruct(*wide), jax.ShapeDtypeStruct(*narrow)],
        in_specs=[ANY] * (expert_count + 2),
        out_specs=[ANY, ANY],
        scratch_shapes=[
            pltpu.VMEM(*wide),
            pltpu.VMEM(*narrow),
            pltpu.SemaphoreType.DMA((expert_count,)),
            pltpu.SemaphoreType.DMA((2,)),
            pltpu.SemaphoreType.DMA((2,)),
        ],
        compiler_params=pltpu.CompilerParams(vmem_limit_bytes=VMEM_LIMIT // 4),
    )(*in_hbm(pieces), *in_hbm(hidden))
    grad_keep, grad_send, dgate, dup, rows_scaled = expert_call(
        functools.partial(backward_kernel, rows, expert_count),
        [half_wide, half_wide, narrow, narrow, wide],
        held + [narrow, narrow, wide],
        [expert_count, expert_count, 4, 7],
        flops,
        [where, *gate_pre, *up_pre, *pieces, *weights],
    )
    out_came, grad_keep, grad_send, dgate, dup, rows_scaled = tie(
        (out_came, grad_keep, grad_send, dgate, dup, rows_scaled)
    )
    grad_came = swap_inner(grad_send, SECOND)
    out_column = reduce_part(out_keep.reshape(2, -1, width), out_came)
    grad_came, out_column, dgate, dup, rows_scaled, hidden, rows_in = tie(
        (grad_came, out_column, dgate, dup, rows_scaled, hidden, rows_in)
    )

    def half(value, which, size):
        return lax.dynamic_slice_in_dim(value, which * size, size, 1)

    other = 1 - replica
    sent = (
        contract_rows(half(rows_in, other, half_width), dgate).astype(bf16),
        contract_rows(half(rows_in, other, half_width), dup).astype(bf16),
        contract_rows(half(hidden, other, half_hidden), rows_scaled).astype(bf16),
    )
    back = partner_2(sent, "rep", 0)
    gate_out = add_bf16(contract_rows(half(rows_in, replica, half_width), dgate), back[0])
    up_out = add_bf16(contract_rows(half(rows_in, replica, half_width), dup), back[1])
    down_out = add_bf16(contract_rows(half(hidden, replica, half_hidden), rows_scaled), back[2])
    masks = [2**bit for bit in range(lax.axis_size("grp").bit_length() - 1)]
    out_column = halve_column(out_column, masks[:-1])
    half = out_column.shape[0] // 2
    out_terms = [out_column[:half], swap_group(out_column[half:], masks[-1])]
    grad_column = reduce_part(grad_keep.reshape(2, -1, width), grad_came)
    grad_terms = send_column(grad_column)
    out_terms, grad_terms[1], gate_out, up_out, down_out = tie(
        (out_terms, grad_terms[1], gate_out, up_out, down_out)
    )
    layer_out, token_grad = add_all(out_terms), add_all(grad_terms)
    return layer_out, token_grad, gate_out[None], up_out[None], down_out[None]


def solution(mesh):
    in_specs = (
        P(("grp", "exp", "rep"), None),
        P(("grp", "exp", "rep"), None),
        P(("grp", "exp", "rep"), None),
        P(("grp", "exp", "rep"), None),
        P(("grp", "exp"), "rep", None),
        P(("grp", "exp"), "rep", None),
        P(("grp", "exp"), "rep", None),
    )
    out_specs = (
        P(("grp", "exp", "rep"), None),
        P(("grp", "exp", "rep"), None),
        P(("grp", "exp"), "rep", None),
        P(("grp", "exp"), "rep", None),
        P(("grp", "exp"), "rep", None),
    )
    sizes = dict(mesh.shape)
    group_bits = sizes["grp"] & (sizes["grp"] - 1) == 0
    whole_blocks = sizes["exp"] == 4 and sizes["rep"] == 2 and group_bits and sizes["grp"] * sizes["exp"] <= 2 * TOP
    local = dense_local if whole_blocks else routed_local
    return jax.shard_map(local, mesh=mesh, in_specs=in_specs, out_specs=out_specs, check_vma=False)
```

```python
import functools

import jax
import jax.numpy as jnp
from jax import lax
from jax.experimental import pallas as pl
from jax.experimental.pallas import tpu as pltpu
from jax.sharding import PartitionSpec as P

TOP = 8


def partner_2(value, axis, bit):
    mask = 2**bit
    pairs = [(source, source ^ mask) for source in range(lax.axis_size(axis))]
    return lax.ppermute(value, axis, pairs)


def contract_rows(left, right):
    return lax.dot_general(
        left, right, (((0,), (0,)), ((), ())), preferred_element_type=jnp.float32
    )


def contract_cols(left, right):
    return lax.dot_general(
        left, right, (((1,), (1,)), ((), ())), preferred_element_type=jnp.float32
    )


def rounded_sum(first, second):
    left_part = lax.optimization_barrier(first.astype(jnp.bfloat16))
    right_part = lax.optimization_barrier(second.astype(jnp.bfloat16))
    return left_part.astype(jnp.float32) + right_part.astype(jnp.float32)


def routed_local(tokens, cotangent, expert_ids, gate_probs, gate_weight, up_weight, down_weight):
    group_count = lax.axis_size("grp")
    inner_count = lax.axis_size("exp")
    expert_count = group_count * inner_count
    token_count = tokens.shape[0]
    model_width = tokens.shape[1]
    capacity = 3 * token_count * TOP // (2 * expert_count)
    slot_count = expert_count * capacity
    row_count = token_count * TOP
    flat_ids = expert_ids.reshape(row_count)
    flat_probs = gate_probs.reshape(row_count)
    one_hot = (flat_ids[:, None] == jnp.arange(expert_count, dtype=jnp.int32)[None, :]).astype(
        jnp.float32
    )
    earlier = (jnp.arange(row_count)[:, None] > jnp.arange(row_count)[None, :]).astype(jnp.float32)
    counted = jnp.dot(earlier, one_hot, precision=lax.Precision.HIGHEST)
    slot_rank = jnp.sum(counted * one_hot, axis=1).astype(jnp.int32)
    target = flat_ids * capacity + slot_rank
    picked = jnp.arange(slot_count, dtype=jnp.int32)[:, None] == target[None, :]
    slot_probs = jnp.dot(picked.astype(jnp.float32), flat_probs, precision=lax.Precision.HIGHEST)
    pick_tokens = picked.reshape(slot_count, token_count, TOP).any(axis=2).astype(jnp.bfloat16)
    send_tokens = jnp.dot(pick_tokens, tokens, preferred_element_type=jnp.float32).astype(
        jnp.bfloat16
    )
    send_scaled = (
        jnp.dot(pick_tokens, cotangent, preferred_element_type=jnp.float32) * slot_probs[:, None]
    ).astype(jnp.bfloat16)
    whole = (
        lax.all_gather(gate_weight, "rep", axis=1, tiled=True),
        lax.all_gather(up_weight, "rep", axis=1, tiled=True),
        lax.all_gather(down_weight, "rep", axis=1, tiled=True),
    )
    gate_mat = whole[0][0]
    up_mat = whole[1][0]
    down_mat = whole[2][0]
    arrived = (
        lax.all_to_all(
            send_tokens.reshape(expert_count, capacity, model_width),
            ("grp", "exp"),
            split_axis=0,
            concat_axis=0,
            tiled=True,
        ),
        lax.all_to_all(
            send_scaled.reshape(expert_count, capacity, model_width),
            ("grp", "exp"),
            split_axis=0,
            concat_axis=0,
            tiled=True,
        ),
    )
    rows_in = arrived[0].reshape(slot_count, model_width)
    rows_scaled = arrived[1].reshape(slot_count, model_width)
    gate_pre = jnp.dot(rows_in, gate_mat, preferred_element_type=jnp.float32)
    up_pre = jnp.dot(rows_in, up_mat, preferred_element_type=jnp.float32)
    sigma = jax.nn.sigmoid(gate_pre)
    act = gate_pre * sigma
    hidden = (act * up_pre).astype(jnp.bfloat16)
    out_rows = jnp.dot(hidden, down_mat, preferred_element_type=jnp.float32).astype(jnp.bfloat16)
    dhidden = contract_cols(rows_scaled, down_mat)
    dgate = (dhidden * up_pre * sigma * (1.0 + gate_pre * (1.0 - sigma))).astype(jnp.bfloat16)
    dup = (dhidden * act).astype(jnp.bfloat16)
    grad_rows = (contract_cols(dgate, gate_mat) + contract_cols(dup, up_mat)).astype(jnp.bfloat16)
    returned = (
        lax.all_to_all(
            out_rows.reshape(expert_count, capacity, model_width),
            ("grp", "exp"),
            split_axis=0,
            concat_axis=0,
            tiled=True,
        ),
        lax.all_to_all(
            grad_rows.reshape(expert_count, capacity, model_width),
            ("grp", "exp"),
            split_axis=0,
            concat_axis=0,
            tiled=True,
        ),
    )
    replica = lax.axis_index("rep")
    other = 1 - replica
    half_width = gate_weight.shape[1]
    half_hidden = down_weight.shape[1]
    own_in = lax.dynamic_slice_in_dim(rows_in, replica * half_width, half_width, 1)
    own_hidden = lax.dynamic_slice_in_dim(hidden, replica * half_hidden, half_hidden, 1)
    send_in = lax.dynamic_slice_in_dim(rows_in, other * half_width, half_width, 1)
    send_hidden = lax.dynamic_slice_in_dim(hidden, other * half_hidden, half_hidden, 1)
    partner = partner_2((send_in, rows_scaled, send_hidden, dgate, dup), "rep", 0)
    gate_out = rounded_sum(contract_rows(own_in, dgate), contract_rows(partner[0], partner[3]))[
        None
    ]
    up_out = rounded_sum(contract_rows(own_in, dup), contract_rows(partner[0], partner[4]))[None]
    down_out = rounded_sum(
        contract_rows(own_hidden, rows_scaled), contract_rows(partner[2], partner[1])
    )[None]
    back_out = returned[0].reshape(slot_count, model_width)
    back_grad = returned[1].reshape(slot_count, model_width)
    route_out = jnp.dot(picked.T.astype(jnp.bfloat16), back_out, preferred_element_type=jnp.float32)
    layer_out = jnp.sum(
        route_out.reshape(token_count, TOP, model_width) * gate_probs[:, :, None], axis=1
    )
    token_grad = jnp.dot(pick_tokens.T, back_grad, preferred_element_type=jnp.float32)
    return (
        layer_out.astype(jnp.bfloat16),
        token_grad.astype(jnp.bfloat16),
        gate_out.astype(jnp.bfloat16),
        up_out.astype(jnp.bfloat16),
        down_out.astype(jnp.bfloat16),
    )


FIRST, SECOND = (1, 2), (2, 1)
tie = lax.optimization_barrier
VMEM_LIMIT = 32 * 2**20
ANY = pl.BlockSpec(memory_space=pl.ANY)
VMEM = pl.BlockSpec(memory_space=pltpu.VMEM)
SMEM = pl.BlockSpec(memory_space=pltpu.SMEM)


def swap_group(value, mask):
    count = lax.axis_size("grp")
    return lax.ppermute(value, "grp", [(i, i ^ mask) for i in range(count)])


def swap_inner(value, masks):
    inner, reps = lax.axis_size("exp"), lax.axis_size("rep")
    pairs = [
        (e * reps + r, (e ^ masks[r]) * reps + r) for e in range(inner) for r in range(reps)
    ]
    return lax.ppermute(value, ("exp", "rep"), pairs)


def steps_of(count):
    steps = [0]
    while len(steps) < count:
        steps = [2 * step for step in steps] + [2 * step + 1 for step in steps]
    return steps


def gather_blocks(block, beside):
    count = lax.axis_size("grp")
    moved, first, second, both = {0: block, 1: swap_group(block, 1)}, {}, {}, {}
    for k in range(count + 1):
        due = [
            (part, step)
            for part, step in ((moved, k), (first, k - 1), (second, k - 2), (both, k - 2))
            if k > 0 and step in part
        ]
        values = beside(k, [part[step] for part, step in due])
        for (part, step), value in zip(due, values):
            part[step] = value
        if k == 0:
            mask = 2
            while mask < count:
                moved[mask] = swap_group(moved[0], mask)
                mask *= 2
        if k < count:
            mask = 1
            while mask < (k & -k):
                moved[k | mask] = swap_group(moved[k], mask)
                mask *= 2
            first[k] = swap_inner(moved[k], FIRST)
            second[k] = swap_group(second[k - 1], 1) if k in (3,) else swap_inner(moved[k], SECOND)
        if k - 1 in ():
            both[k - 1] = swap_group(both[k - 2], 1)
        elif k > 0:
            both[k - 1] = swap_inner(first[k - 1], SECOND)
    return [part[step] for part in (moved, first, second, both) for step in steps_of(count)]


def add_bf16(left, right):
    return (left.astype(jnp.float32) + right.astype(jnp.float32)).astype(jnp.bfloat16)


def reduce_part(here, came):
    came = came.reshape(here.shape)
    passed = swap_inner(add_bf16(here[1], came[1]), FIRST)
    return add_bf16(here[0].astype(jnp.float32) + came[0].astype(jnp.float32), passed)


def send_column(column):
    count = lax.axis_size("grp")
    rows = column.shape[0] // count
    return [
        column[q * rows : (q + 1) * rows] if step == 0
        else swap_group(column[q * rows : (q + 1) * rows], step)
        for q, step in enumerate(steps_of(count))
    ]


def halve_column(column, masks):
    for mask in masks:
        half = column.shape[0] // 2
        column = add_bf16(column[:half], swap_group(column[half:], mask))
    return column


def add_all(values):
    total = values[0].astype(jnp.float32)
    for value in values[1:]:
        total = total + value.astype(jnp.float32)
    return total.astype(jnp.bfloat16)


def token_block(tokens, cotangent, expert_ids, gate_probs, expert_count):
    named = expert_ids[:, :, None] == jnp.arange(expert_count, dtype=jnp.int32)
    rest = jnp.sum(jnp.where(named, gate_probs[:, :, None], 0.0), axis=1)
    terms = []
    for _ in range(3):
        terms.append(lax.reduce_precision(rest, exponent_bits=8, mantissa_bits=7))
        rest = rest - terms[-1]
    terms = jnp.concatenate(terms, axis=1).astype(jnp.bfloat16)
    rows, side = tokens.shape[0], side_width(expert_count)
    terms = jnp.pad(terms, ((0, rows), (0, side - terms.shape[1])))
    return jnp.concatenate([jnp.concatenate([tokens, cotangent], axis=0), terms], axis=1)


def side_width(expert_count):
    return -(-3 * expert_count // 128) * 128


def start_halves(halves, whole, sems, first_sem, replica):
    own, partner = halves
    size = own.shape[0]
    copies = []
    for k, (half, which) in enumerate(((own, replica), (partner, 1 - replica))):
        place = pl.ds(pl.multiple_of(which * size, size), size)
        copies.append(pltpu.make_async_copy(half, whole.at[place, :], sems.at[first_sem + k]))
        copies[-1].start()
    return copies


def start_rows(pieces, whole, offset, rows, first_col, sems):
    copies = []
    for k, piece in enumerate(pieces):
        part = piece.at[pl.ds(offset, rows), pl.ds(first_col, whole.shape[1])]
        copies.append(pltpu.make_async_copy(part, whole.at[pl.ds(k * rows, rows), :], sems.at[k]))
        copies[-1].start()
    return copies


def start_out(sources_and_places, sems, first_sem):
    copies = []
    for k, (source, place) in enumerate(sources_and_places):
        copies.append(pltpu.make_async_copy(source, place, sems.at[first_sem + k]))
        copies[-1].start()
    return copies


def start_parts(parts, whole, sems, first_sem):
    size = parts[0].shape[0]
    places = [whole.at[pl.ds(k * size, size), :] for k in range(len(parts))]
    return start_out(list(zip(parts, places)), sems, first_sem)


def wait_all(copies):
    for copy in copies:
        copy.wait()


def weights_of(side_ref, expert, expert_count):
    lane = lax.broadcasted_iota(jnp.int32, side_ref.shape, 1)
    mine = (lane == expert) | (lane == expert + expert_count) | (lane == expert + 2 * expert_count)
    return jnp.sum(jnp.where(mine, side_ref[...].astype(jnp.float32), 0.0), axis=1, keepdims=True)


def halves_of(whole, cols, keep, send):
    half = keep.shape[0]
    return [
        (whole.at[pl.ds(0, half), cols], keep.at[:, cols]),
        (whole.at[pl.ds(half, half), cols], send.at[:, cols]),
    ]


def tiles(size, count):
    return [pl.ds(i * size // count, size // count) for i in range(count)]


def assemble_kernel(rows, count, *refs):
    pieces, halves, refs = refs[:count], refs[count : count + 2], refs[count + 2 :]
    whole_out, hidden_out, whole, hidden, sems, half_sems, out_sems = refs
    copies = start_rows(pieces, whole, 0, rows, 0, sems)
    wait_all(copies + start_parts(halves, hidden, half_sems, 0))
    wait_all(start_out([(whole, whole_out), (hidden, hidden_out)], out_sems, 0))


def weights_kernel(where_ref, *refs):
    wholes, where_out, sems = refs[6:9], refs[9], refs[10]
    copies = []
    for k, whole in enumerate(wholes):
        copies += start_halves(refs[2 * k : 2 * k + 2], whole, sems, 2 * k, where_ref[0])
    for k in range(where_out.shape[0]):
        where_out[k] = where_ref[k]
    wait_all(copies)


def forward_kernel(rows, count, expert_count, where_ref, *refs):
    pieces, refs = refs[:count], refs[count:]
    gate_all, up_all, down_all = refs[0:3]
    whole_out, gate_pre_out, up_pre_out, hidden_out = refs[3:7]
    rows_in, side, gate_pre, up_pre, hidden, out = refs[7:13]
    row_sems, side_sems, out_sems = refs[13:]
    width = rows_in.shape[1]
    row_copies = start_rows(pieces, rows_in, 0, rows, 0, row_sems)
    side_copies = start_rows(pieces, side, 0, rows, width, side_sems)
    wait_all(row_copies)
    pre = jnp.dot(rows_in[...], gate_all[...], preferred_element_type=jnp.float32)
    gate_pre[...] = pre.astype(gate_pre.dtype)
    act = pre * jax.nn.sigmoid(pre)
    pre = jnp.dot(rows_in[...], up_all[...], preferred_element_type=jnp.float32)
    up_pre[...] = pre.astype(up_pre.dtype)
    hidden[...] = (act * pre).astype(jnp.bfloat16)
    outs = start_out(
        [(gate_pre, gate_pre_out), (up_pre, up_pre_out), (hidden, hidden_out)], out_sems, 0
    )
    wait_all(side_copies)
    probs = weights_of(side, where_ref[1], expert_count)
    for t, cols in enumerate(tiles(width, 2)):
        part = jnp.dot(hidden[...], down_all[:, cols], preferred_element_type=jnp.float32)
        out[:, cols] = (part * probs).astype(jnp.bfloat16)
        outs += start_out([(out.at[:, cols], whole_out.at[:, cols])], out_sems, 3 + t)
    wait_all(outs)


def backward_kernel(rows, count, where_ref, *refs):
    gate_pre_in, up_pre_in, refs = refs[0:2], refs[2:4], refs[4:]
    pieces, refs = refs[:count], refs[count:]
    gate_all, up_all, down_all = refs[0:3]
    keep, send, dgate_out, dup_out, scaled_out = refs[3:8]
    scaled, side, gate_pre, up_pre, dgate, dup, grad = refs[8:15]
    row_sems, side_sems, pre_sems, out_sems = refs[15:]
    width = scaled.shape[1]
    row_copies = start_rows(pieces, scaled, rows, rows, 0, row_sems)
    side_copies = start_rows(pieces, side, 0, rows, width, side_sems)
    pre_copies = start_parts(gate_pre_in, gate_pre, pre_sems, 0)
    pre_copies += start_parts(up_pre_in, up_pre, pre_sems, 2)
    wait_all(row_copies + side_copies)
    probs = weights_of(side, where_ref[1], count)
    scaled[...] = (scaled[...].astype(jnp.float32) * probs).astype(jnp.bfloat16)
    outs = start_out([(scaled, scaled_out)], out_sems, 0)
    dhidden = contract_cols(scaled[...], down_all[...])
    wait_all(pre_copies)
    pre, gain = gate_pre[...].astype(jnp.float32), up_pre[...].astype(jnp.float32)
    sigma = jax.nn.sigmoid(pre)
    dgate[...] = (dhidden * gain * sigma * (1.0 + pre * (1.0 - sigma))).astype(jnp.bfloat16)
    dup[...] = (dhidden * (pre * sigma)).astype(jnp.bfloat16)
    outs += start_out([(dgate, dgate_out), (dup, dup_out)], out_sems, 1)
    for t, cols in enumerate(tiles(width, 2)):
        part = contract_cols(dgate[...], gate_all[cols, :])
        grad[:, cols] = (part + contract_cols(dup[...], up_all[cols, :])).astype(jnp.bfloat16)
        outs += start_out(halves_of(grad, cols, keep, send), out_sems, 3 + 2 * t)
    wait_all(outs)


def in_hbm(values):
    return [pltpu.with_memory_space_constraint(value, pltpu.HBM) for value in values]


def expert_call(kernel, outs, scratch, sems, flops, inputs):
    return pl.pallas_call(
        kernel,
        out_shape=[pltpu.HBM(shape, dtype) for shape, dtype in outs],
        in_specs=[SMEM] + [ANY] * (len(inputs) - 4) + [VMEM] * 3,
        out_specs=[ANY] * len(outs),
        scratch_shapes=[pltpu.VMEM(shape, dtype) for shape, dtype in scratch]
        + [pltpu.SemaphoreType.DMA((n,)) for n in sems],
        compiler_params=pltpu.CompilerParams(vmem_limit_bytes=VMEM_LIMIT),
        cost_estimate=pl.CostEstimate(
            flops=flops,
            bytes_accessed=sum(2 * value.size for value in inputs),
            transcendentals=0,
        ),
    )(inputs[0], *in_hbm(inputs[1:-3]), *inputs[-3:])


class WholeWeights:
    def __init__(self, own, where):
        self.own, self.where, self.came, self.whole = list(own), where, [], None

    def load(self):
        width, hidden_width = 2 * self.own[0].shape[0], self.own[0].shape[1]
        shapes = [(width, hidden_width), (width, hidden_width), (hidden_width, width)]
        halves = [value for pair in zip(self.own, self.came) for value in pair]
        *self.whole, self.where = pl.pallas_call(
            weights_kernel,
            out_shape=[pltpu.VMEM(shape, jnp.bfloat16) for shape in shapes]
            + [jax.ShapeDtypeStruct(self.where.shape, self.where.dtype)],
            in_specs=[SMEM] + [ANY] * 6,
            out_specs=[VMEM] * 3 + [SMEM],
            scratch_shapes=[pltpu.SemaphoreType.DMA((6,))],
            compiler_params=pltpu.CompilerParams(vmem_limit_bytes=VMEM_LIMIT),
        )(self.where, *in_hbm(halves))
        self.whole = [pltpu.with_memory_space_constraint(w, pltpu.VMEM) for w in self.whole]

    def __call__(self, step, values):
        if not values:
            return values
        count = len(values)
        if step <= 2:
            new = self.own[:1] if step == 1 else self.own[1:]
            values = list(tie((*values, *new)))
            self.came += [partner_2(value, "rep", 0) for value in values[count:]]
        elif self.whole is None:
            self.load()
            *values, self.where = tie((*values, self.where))
        return values[:count]


def dense_local(tokens, cotangent, expert_ids, gate_probs, gate_weight, up_weight, down_weight):
    expert_count = lax.axis_size("grp") * lax.axis_size("exp")
    replica = lax.axis_index("rep")
    rows, width = tokens.shape
    half_width, hidden_width = gate_weight.shape[1:]
    half_hidden = down_weight.shape[1]
    total = expert_count * rows
    own = (gate_weight[0], up_weight[0], down_weight[0])
    expert = lax.axis_index("grp") * lax.axis_size("exp") + lax.axis_index("exp")
    where = jnp.stack([replica, expert]).astype(jnp.int32)
    block = token_block(tokens, cotangent, expert_ids, gate_probs, expert_count)
    collected = WholeWeights(own, where)
    pieces = gather_blocks(block, collected)
    if collected.whole is None:
        collected.load()
    weights, where = collected.whole, collected.where
    bf16 = jnp.bfloat16
    wide, narrow = ((total, width), bf16), ((total, hidden_width), bf16)
    half_wide = ((total // 2, width), bf16)
    half_narrow = ((total // 2, hidden_width), bf16)
    side = side_width(expert_count)
    flops = 6 * total * width * hidden_width
    half_count = expert_count // 2
    forward, waiting = [], pieces[half_count:]
    for half_pieces in (pieces[:half_count], None):
        forward.append(
            list(expert_call(
                functools.partial(forward_kernel, rows, half_count, expert_count),
                [half_wide] + [half_narrow] * 3,
                [half_wide, ((total // 2, side), bf16)] + [half_narrow] * 3 + [half_wide],
                [half_count, half_count, 5],
                flops // 2,
                [where, *(half_pieces or waiting), *weights],
            ))
        )
        if half_pieces:
            forward[0][0], waiting = tie((forward[0][0], waiting))
    (out_keep, out_send), gate_pre, up_pre, hidden = zip(*forward)
    held = [wide, ((total, side), bf16), narrow, narrow]
    out_came = swap_inner(out_send, SECOND)
    rows_in, hidden = pl.pallas_call(
        functools.partial(assemble_kernel, rows, expert_count),
        out_shape=[jax.ShapeDtypeStruct(*wide), jax.ShapeDtypeStruct(*narrow)],
        in_specs=[ANY] * (expert_count + 2),
        out_specs=[ANY, ANY],
        scratch_shapes=[
            pltpu.VMEM(*wide),
            pltpu.VMEM(*narrow),
            pltpu.SemaphoreType.DMA((expert_count,)),
            pltpu.SemaphoreType.DMA((2,)),
            pltpu.SemaphoreType.DMA((2,)),
        ],
        compiler_params=pltpu.CompilerParams(vmem_limit_bytes=VMEM_LIMIT // 4),
    )(*in_hbm(pieces), *in_hbm(hidden))
    grad_keep, grad_send, dgate, dup, rows_scaled = expert_call(
        functools.partial(backward_kernel, rows, expert_count),
        [half_wide, half_wide, narrow, narrow, wide],
        held + [narrow, narrow, wide],
        [expert_count, expert_count, 4, 7],
        flops,
        [where, *gate_pre, *up_pre, *pieces, *weights],
    )
    grad_came = swap_inner(grad_send, SECOND)
    out_column = reduce_part(out_keep.reshape(2, -1, width), out_came)
    grad_came, out_column, dgate, dup, rows_scaled, hidden, rows_in = tie(
        (grad_came, out_column, dgate, dup, rows_scaled, hidden, rows_in)
    )

    def half(value, which, size):
        return lax.dynamic_slice_in_dim(value, which * size, size, 1)

    other = 1 - replica
    sent = (
        contract_rows(half(rows_in, other, half_width), dgate).astype(bf16),
        contract_rows(half(rows_in, other, half_width), dup).astype(bf16),
        contract_rows(half(hidden, other, half_hidden), rows_scaled).astype(bf16),
    )
    back = partner_2(sent, "rep", 0)
    gate_out = add_bf16(contract_rows(half(rows_in, replica, half_width), dgate), back[0])
    up_out = add_bf16(contract_rows(half(rows_in, replica, half_width), dup), back[1])
    down_out = add_bf16(contract_rows(half(hidden, replica, half_hidden), rows_scaled), back[2])
    masks = [2**bit for bit in range(lax.axis_size("grp").bit_length() - 1)]
    out_column = halve_column(out_column, masks[:-1])
    half = out_column.shape[0] // 2
    out_terms = [out_column[:half], swap_group(out_column[half:], masks[-1])]
    grad_column = reduce_part(grad_keep.reshape(2, -1, width), grad_came)
    grad_terms = send_column(grad_column)
    out_terms, grad_terms[1], gate_out, up_out, down_out = tie(
        (out_terms, grad_terms[1], gate_out, up_out, down_out)
    )
    layer_out, token_grad = add_all(out_terms), add_all(grad_terms)
    return layer_out, token_grad, gate_out[None], up_out[None], down_out[None]


def solution(mesh):
    in_specs = (
        P(("grp", "exp", "rep"), None),
        P(("grp", "exp", "rep"), None),
        P(("grp", "exp", "rep"), None),
        P(("grp", "exp", "rep"), None),
        P(("grp", "exp"), "rep", None),
        P(("grp", "exp"), "rep", None),
        P(("grp", "exp"), "rep", None),
    )
    out_specs = (
        P(("grp", "exp", "rep"), None),
        P(("grp", "exp", "rep"), None),
        P(("grp", "exp"), "rep", None),
        P(("grp", "exp"), "rep", None),
        P(("grp", "exp"), "rep", None),
    )
    sizes = dict(mesh.shape)
    group_bits = sizes["grp"] & (sizes["grp"] - 1) == 0
    whole_blocks = sizes["exp"] == 4 and sizes["rep"] == 2 and group_bits and sizes["grp"] * sizes["exp"] <= 2 * TOP
    local = dense_local if whole_blocks else routed_local
    return jax.shard_map(local, mesh=mesh, in_specs=in_specs, out_specs=out_specs, check_vma=False)
```

```python
import functools

import jax
import jax.numpy as jnp
from jax import lax
from jax.experimental import pallas as pl
from jax.experimental.pallas import tpu as pltpu
from jax.sharding import PartitionSpec as P

TOP = 8


def partner_2(value, axis, bit):
    mask = 2**bit
    pairs = [(source, source ^ mask) for source in range(lax.axis_size(axis))]
    return lax.ppermute(value, axis, pairs)


def contract_rows(left, right):
    return lax.dot_general(
        left, right, (((0,), (0,)), ((), ())), preferred_element_type=jnp.float32
    )


def contract_cols(left, right):
    return lax.dot_general(
        left, right, (((1,), (1,)), ((), ())), preferred_element_type=jnp.float32
    )


def rounded_sum(first, second):
    left_part = lax.optimization_barrier(first.astype(jnp.bfloat16))
    right_part = lax.optimization_barrier(second.astype(jnp.bfloat16))
    return left_part.astype(jnp.float32) + right_part.astype(jnp.float32)


def routed_local(tokens, cotangent, expert_ids, gate_probs, gate_weight, up_weight, down_weight):
    group_count = lax.axis_size("grp")
    inner_count = lax.axis_size("exp")
    expert_count = group_count * inner_count
    token_count = tokens.shape[0]
    model_width = tokens.shape[1]
    capacity = 3 * token_count * TOP // (2 * expert_count)
    slot_count = expert_count * capacity
    row_count = token_count * TOP
    flat_ids = expert_ids.reshape(row_count)
    flat_probs = gate_probs.reshape(row_count)
    one_hot = (flat_ids[:, None] == jnp.arange(expert_count, dtype=jnp.int32)[None, :]).astype(
        jnp.float32
    )
    earlier = (jnp.arange(row_count)[:, None] > jnp.arange(row_count)[None, :]).astype(jnp.float32)
    counted = jnp.dot(earlier, one_hot, precision=lax.Precision.HIGHEST)
    slot_rank = jnp.sum(counted * one_hot, axis=1).astype(jnp.int32)
    target = flat_ids * capacity + slot_rank
    picked = jnp.arange(slot_count, dtype=jnp.int32)[:, None] == target[None, :]
    slot_probs = jnp.dot(picked.astype(jnp.float32), flat_probs, precision=lax.Precision.HIGHEST)
    pick_tokens = picked.reshape(slot_count, token_count, TOP).any(axis=2).astype(jnp.bfloat16)
    send_tokens = jnp.dot(pick_tokens, tokens, preferred_element_type=jnp.float32).astype(
        jnp.bfloat16
    )
    send_scaled = (
        jnp.dot(pick_tokens, cotangent, preferred_element_type=jnp.float32) * slot_probs[:, None]
    ).astype(jnp.bfloat16)
    whole = (
        lax.all_gather(gate_weight, "rep", axis=1, tiled=True),
        lax.all_gather(up_weight, "rep", axis=1, tiled=True),
        lax.all_gather(down_weight, "rep", axis=1, tiled=True),
    )
    gate_mat = whole[0][0]
    up_mat = whole[1][0]
    down_mat = whole[2][0]
    arrived = (
        lax.all_to_all(
            send_tokens.reshape(expert_count, capacity, model_width),
            ("grp", "exp"),
            split_axis=0,
            concat_axis=0,
            tiled=True,
        ),
        lax.all_to_all(
            send_scaled.reshape(expert_count, capacity, model_width),
            ("grp", "exp"),
            split_axis=0,
            concat_axis=0,
            tiled=True,
        ),
    )
    rows_in = arrived[0].reshape(slot_count, model_width)
    rows_scaled = arrived[1].reshape(slot_count, model_width)
    gate_pre = jnp.dot(rows_in, gate_mat, preferred_element_type=jnp.float32)
    up_pre = jnp.dot(rows_in, up_mat, preferred_element_type=jnp.float32)
    sigma = jax.nn.sigmoid(gate_pre)
    act = gate_pre * sigma
    hidden = (act * up_pre).astype(jnp.bfloat16)
    out_rows = jnp.dot(hidden, down_mat, preferred_element_type=jnp.float32).astype(jnp.bfloat16)
    dhidden = contract_cols(rows_scaled, down_mat)
    dgate = (dhidden * up_pre * sigma * (1.0 + gate_pre * (1.0 - sigma))).astype(jnp.bfloat16)
    dup = (dhidden * act).astype(jnp.bfloat16)
    grad_rows = (contract_cols(dgate, gate_mat) + contract_cols(dup, up_mat)).astype(jnp.bfloat16)
    returned = (
        lax.all_to_all(
            out_rows.reshape(expert_count, capacity, model_width),
            ("grp", "exp"),
            split_axis=0,
            concat_axis=0,
            tiled=True,
        ),
        lax.all_to_all(
            grad_rows.reshape(expert_count, capacity, model_width),
            ("grp", "exp"),
            split_axis=0,
            concat_axis=0,
            tiled=True,
        ),
    )
    replica = lax.axis_index("rep")
    other = 1 - replica
    half_width = gate_weight.shape[1]
    half_hidden = down_weight.shape[1]
    own_in = lax.dynamic_slice_in_dim(rows_in, replica * half_width, half_width, 1)
    own_hidden = lax.dynamic_slice_in_dim(hidden, replica * half_hidden, half_hidden, 1)
    send_in = lax.dynamic_slice_in_dim(rows_in, other * half_width, half_width, 1)
    send_hidden = lax.dynamic_slice_in_dim(hidden, other * half_hidden, half_hidden, 1)
    partner = partner_2((send_in, rows_scaled, send_hidden, dgate, dup), "rep", 0)
    gate_out = rounded_sum(contract_rows(own_in, dgate), contract_rows(partner[0], partner[3]))[
        None
    ]
    up_out = rounded_sum(contract_rows(own_in, dup), contract_rows(partner[0], partner[4]))[None]
    down_out = rounded_sum(
        contract_rows(own_hidden, rows_scaled), contract_rows(partner[2], partner[1])
    )[None]
    back_out = returned[0].reshape(slot_count, model_width)
    back_grad = returned[1].reshape(slot_count, model_width)
    route_out = jnp.dot(picked.T.astype(jnp.bfloat16), back_out, preferred_element_type=jnp.float32)
    layer_out = jnp.sum(
        route_out.reshape(token_count, TOP, model_width) * gate_probs[:, :, None], axis=1
    )
    token_grad = jnp.dot(pick_tokens.T, back_grad, preferred_element_type=jnp.float32)
    return (
        layer_out.astype(jnp.bfloat16),
        token_grad.astype(jnp.bfloat16),
        gate_out.astype(jnp.bfloat16),
        up_out.astype(jnp.bfloat16),
        down_out.astype(jnp.bfloat16),
    )


FIRST, SECOND = (1, 2), (2, 1)
tie = lax.optimization_barrier
VMEM_LIMIT = 32 * 2**20
ANY = pl.BlockSpec(memory_space=pl.ANY)
VMEM = pl.BlockSpec(memory_space=pltpu.VMEM)
SMEM = pl.BlockSpec(memory_space=pltpu.SMEM)


def swap_group(value, mask):
    count = lax.axis_size("grp")
    return lax.ppermute(value, "grp", [(i, i ^ mask) for i in range(count)])


def swap_inner(value, masks):
    inner, reps = lax.axis_size("exp"), lax.axis_size("rep")
    pairs = [
        (e * reps + r, (e ^ masks[r]) * reps + r) for e in range(inner) for r in range(reps)
    ]
    return lax.ppermute(value, ("exp", "rep"), pairs)


def steps_of(count):
    steps = [0]
    while len(steps) < count:
        steps = [2 * step for step in steps] + [2 * step + 1 for step in steps]
    return steps


def gather_blocks(block, beside):
    count = lax.axis_size("grp")
    moved, first, second, both = {0: block, 1: swap_group(block, 1)}, {}, {}, {}
    for k in range(count + 1):
        due = [
            (part, step)
            for part, step in ((moved, k), (first, k - 1), (second, k - 2), (both, k - 2))
            if k > 0 and step in part
        ]
        values = beside(k, [part[step] for part, step in due])
        for (part, step), value in zip(due, values):
            part[step] = value
        if k == 0:
            mask = 2
            while mask < count:
                moved[mask] = swap_group(moved[0], mask)
                mask *= 2
        if k < count:
            mask = 1
            while mask < (k & -k):
                moved[k | mask] = swap_group(moved[k], mask)
                mask *= 2
            first[k] = swap_inner(moved[k], FIRST)
            second[k] = swap_group(second[k - 1], 1) if k in (3,) else swap_inner(moved[k], SECOND)
        if k - 1 in ():
            both[k - 1] = swap_group(both[k - 2], 1)
        elif k > 0:
            both[k - 1] = swap_inner(first[k - 1], SECOND)
    return [part[step] for part in (moved, first, second, both) for step in steps_of(count)]


def add_bf16(left, right):
    return (left.astype(jnp.float32) + right.astype(jnp.float32)).astype(jnp.bfloat16)


def reduce_part(here, came):
    came = came.reshape(here.shape)
    passed = swap_inner(add_bf16(here[1], came[1]), FIRST)
    return add_bf16(here[0].astype(jnp.float32) + came[0].astype(jnp.float32), passed)


def send_column(column):
    count = lax.axis_size("grp")
    rows = column.shape[0] // count
    return [
        column[q * rows : (q + 1) * rows] if step == 0
        else swap_group(column[q * rows : (q + 1) * rows], step)
        for q, step in enumerate(steps_of(count))
    ]


def halve_column(column, masks):
    for mask in masks:
        half = column.shape[0] // 2
        column = add_bf16(column[:half], swap_group(column[half:], mask))
    return column


def add_all(values):
    total = values[0].astype(jnp.float32)
    for value in values[1:]:
        total = total + value.astype(jnp.float32)
    return total.astype(jnp.bfloat16)


def token_block(tokens, cotangent, expert_ids, gate_probs, expert_count):
    named = expert_ids[:, :, None] == jnp.arange(expert_count, dtype=jnp.int32)
    rest = jnp.sum(jnp.where(named, gate_probs[:, :, None], 0.0), axis=1)
    terms = []
    for _ in range(3):
        terms.append(lax.reduce_precision(rest, exponent_bits=8, mantissa_bits=7))
        rest = rest - terms[-1]
    terms = jnp.concatenate(terms, axis=1).astype(jnp.bfloat16)
    rows, side = tokens.shape[0], side_width(expert_count)
    terms = jnp.pad(terms, ((0, rows), (0, side - terms.shape[1])))
    return jnp.concatenate([jnp.concatenate([tokens, cotangent], axis=0), terms], axis=1)


def side_width(expert_count):
    return -(-3 * expert_count // 128) * 128


def start_halves(halves, whole, sems, first_sem, replica):
    own, partner = halves
    size = own.shape[0]
    copies = []
    for k, (half, which) in enumerate(((own, replica), (partner, 1 - replica))):
        place = pl.ds(pl.multiple_of(which * size, size), size)
        copies.append(pltpu.make_async_copy(half, whole.at[place, :], sems.at[first_sem + k]))
        copies[-1].start()
    return copies


def start_rows(pieces, whole, offset, rows, first_col, sems):
    copies = []
    for k, piece in enumerate(pieces):
        part = piece.at[pl.ds(offset, rows), pl.ds(first_col, whole.shape[1])]
        copies.append(pltpu.make_async_copy(part, whole.at[pl.ds(k * rows, rows), :], sems.at[k]))
        copies[-1].start()
    return copies


def start_out(sources_and_places, sems, first_sem):
    copies = []
    for k, (source, place) in enumerate(sources_and_places):
        copies.append(pltpu.make_async_copy(source, place, sems.at[first_sem + k]))
        copies[-1].start()
    return copies


def start_parts(parts, whole, sems, first_sem):
    size = parts[0].shape[0]
    places = [whole.at[pl.ds(k * size, size), :] for k in range(len(parts))]
    return start_out(list(zip(parts, places)), sems, first_sem)


def wait_all(copies):
    for copy in copies:
        copy.wait()


def weights_of(side_ref, expert, expert_count):
    lane = lax.broadcasted_iota(jnp.int32, side_ref.shape, 1)
    mine = (lane == expert) | (lane == expert + expert_count) | (lane == expert + 2 * expert_count)
    return jnp.sum(jnp.where(mine, side_ref[...].astype(jnp.float32), 0.0), axis=1, keepdims=True)


def halves_of(whole, cols, keep, send):
    half = keep.shape[0]
    return [
        (whole.at[pl.ds(0, half), cols], keep.at[:, cols]),
        (whole.at[pl.ds(half, half), cols], send.at[:, cols]),
    ]


def tiles(size, count):
    return [pl.ds(i * size // count, size // count) for i in range(count)]


def assemble_kernel(rows, count, *refs):
    pieces, halves, refs = refs[:count], refs[count : count + 2], refs[count + 2 :]
    whole_out, hidden_out, whole, hidden, sems, half_sems, out_sems = refs
    copies = start_rows(pieces, whole, 0, rows, 0, sems)
    wait_all(copies + start_parts(halves, hidden, half_sems, 0))
    wait_all(start_out([(whole, whole_out), (hidden, hidden_out)], out_sems, 0))


def weights_kernel(where_ref, *refs):
    wholes, where_out, sems = refs[6:9], refs[9], refs[10]
    copies = []
    for k, whole in enumerate(wholes):
        copies += start_halves(refs[2 * k : 2 * k + 2], whole, sems, 2 * k, where_ref[0])
    for k in range(where_out.shape[0]):
        where_out[k] = where_ref[k]
    wait_all(copies)


def forward_kernel(rows, count, expert_count, where_ref, *refs):
    pieces, refs = refs[:count], refs[count:]
    gate_all, up_all, down_all = refs[0:3]
    whole_out, gate_pre_out, up_pre_out, hidden_out = refs[3:7]
    rows_in, side, gate_pre, up_pre, hidden, out = refs[7:13]
    row_sems, side_sems, out_sems = refs[13:]
    width = rows_in.shape[1]
    row_copies = start_rows(pieces, rows_in, 0, rows, 0, row_sems)
    side_copies = start_rows(pieces, side, 0, rows, width, side_sems)
    wait_all(row_copies)
    pre = jnp.dot(rows_in[...], gate_all[...], preferred_element_type=jnp.float32)
    gate_pre[...] = pre.astype(gate_pre.dtype)
    act = pre * jax.nn.sigmoid(pre)
    pre = jnp.dot(rows_in[...], up_all[...], preferred_element_type=jnp.float32)
    up_pre[...] = pre.astype(up_pre.dtype)
    hidden[...] = (act * pre).astype(jnp.bfloat16)
    outs = start_out(
        [(gate_pre, gate_pre_out), (up_pre, up_pre_out), (hidden, hidden_out)], out_sems, 0
    )
    wait_all(side_copies)
    probs = weights_of(side, where_ref[1], expert_count)
    for t, cols in enumerate(tiles(width, 2)):
        part = jnp.dot(hidden[...], down_all[:, cols], preferred_element_type=jnp.float32)
        out[:, cols] = (part * probs).astype(jnp.bfloat16)
        outs += start_out([(out.at[:, cols], whole_out.at[:, cols])], out_sems, 3 + t)
    wait_all(outs)


def backward_kernel(rows, count, where_ref, *refs):
    gate_pre_in, up_pre_in, refs = refs[0:2], refs[2:4], refs[4:]
    pieces, refs = refs[:count], refs[count:]
    gate_all, up_all, down_all = refs[0:3]
    keep, send, dgate_out, dup_out, scaled_out = refs[3:8]
    scaled, side, gate_pre, up_pre, dgate, dup, grad = refs[8:15]
    row_sems, side_sems, pre_sems, out_sems = refs[15:]
    width = scaled.shape[1]
    row_copies = start_rows(pieces, scaled, rows, rows, 0, row_sems)
    side_copies = start_rows(pieces, side, 0, rows, width, side_sems)
    pre_copies = start_parts(gate_pre_in, gate_pre, pre_sems, 0)
    pre_copies += start_parts(up_pre_in, up_pre, pre_sems, 2)
    wait_all(row_copies + side_copies)
    probs = weights_of(side, where_ref[1], count)
    scaled[...] = (scaled[...].astype(jnp.float32) * probs).astype(jnp.bfloat16)
    outs = start_out([(scaled, scaled_out)], out_sems, 0)
    dhidden = contract_cols(scaled[...], down_all[...])
    wait_all(pre_copies)
    pre, gain = gate_pre[...].astype(jnp.float32), up_pre[...].astype(jnp.float32)
    sigma = jax.nn.sigmoid(pre)
    dgate[...] = (dhidden * gain * sigma * (1.0 + pre * (1.0 - sigma))).astype(jnp.bfloat16)
    dup[...] = (dhidden * (pre * sigma)).astype(jnp.bfloat16)
    outs += start_out([(dgate, dgate_out), (dup, dup_out)], out_sems, 1)
    for t, cols in enumerate(tiles(width, 2)):
        part = contract_cols(dgate[...], gate_all[cols, :])
        grad[:, cols] = (part + contract_cols(dup[...], up_all[cols, :])).astype(jnp.bfloat16)
        outs += start_out(halves_of(grad, cols, keep, send), out_sems, 3 + 2 * t)
    wait_all(outs)


def in_hbm(values):
    return [pltpu.with_memory_space_constraint(value, pltpu.HBM) for value in values]


def expert_call(kernel, outs, scratch, sems, flops, inputs):
    return pl.pallas_call(
        kernel,
        out_shape=[pltpu.HBM(shape, dtype) for shape, dtype in outs],
        in_specs=[SMEM] + [ANY] * (len(inputs) - 4) + [VMEM] * 3,
        out_specs=[ANY] * len(outs),
        scratch_shapes=[pltpu.VMEM(shape, dtype) for shape, dtype in scratch]
        + [pltpu.SemaphoreType.DMA((n,)) for n in sems],
        compiler_params=pltpu.CompilerParams(vmem_limit_bytes=VMEM_LIMIT),
        cost_estimate=pl.CostEstimate(
            flops=flops,
            bytes_accessed=sum(2 * value.size for value in inputs),
            transcendentals=0,
        ),
    )(inputs[0], *in_hbm(inputs[1:-3]), *inputs[-3:])


class WholeWeights:
    def __init__(self, own, where):
        self.own, self.where, self.came, self.whole = list(own), where, [], None

    def load(self):
        width, hidden_width = 2 * self.own[0].shape[0], self.own[0].shape[1]
        shapes = [(width, hidden_width), (width, hidden_width), (hidden_width, width)]
        halves = [value for pair in zip(self.own, self.came) for value in pair]
        *self.whole, self.where = pl.pallas_call(
            weights_kernel,
            out_shape=[pltpu.VMEM(shape, jnp.bfloat16) for shape in shapes]
            + [jax.ShapeDtypeStruct(self.where.shape, self.where.dtype)],
            in_specs=[SMEM] + [ANY] * 6,
            out_specs=[VMEM] * 3 + [SMEM],
            scratch_shapes=[pltpu.SemaphoreType.DMA((6,))],
            compiler_params=pltpu.CompilerParams(vmem_limit_bytes=VMEM_LIMIT),
        )(self.where, *in_hbm(halves))
        self.whole = [pltpu.with_memory_space_constraint(w, pltpu.VMEM) for w in self.whole]

    def __call__(self, step, values):
        if not values:
            return values
        count = len(values)
        if step <= 2:
            new = self.own[:2] if step == 1 else self.own[2:]
            values = list(tie((*values, *new)))
            self.came += [partner_2(value, "rep", 0) for value in values[count:]]
        elif self.whole is None:
            self.load()
            *values, self.where = tie((*values, self.where))
        return values[:count]


def dense_local(tokens, cotangent, expert_ids, gate_probs, gate_weight, up_weight, down_weight):
    expert_count = lax.axis_size("grp") * lax.axis_size("exp")
    replica = lax.axis_index("rep")
    rows, width = tokens.shape
    half_width, hidden_width = gate_weight.shape[1:]
    half_hidden = down_weight.shape[1]
    total = expert_count * rows
    own = (gate_weight[0], up_weight[0], down_weight[0])
    expert = lax.axis_index("grp") * lax.axis_size("exp") + lax.axis_index("exp")
    where = jnp.stack([replica, expert]).astype(jnp.int32)
    block = token_block(tokens, cotangent, expert_ids, gate_probs, expert_count)
    collected = WholeWeights(own, where)
    pieces = gather_blocks(block, collected)
    if collected.whole is None:
        collected.load()
    weights, where = collected.whole, collected.where
    bf16 = jnp.bfloat16
    wide, narrow = ((total, width), bf16), ((total, hidden_width), bf16)
    half_wide = ((total // 2, width), bf16)
    half_narrow = ((total // 2, hidden_width), bf16)
    side = side_width(expert_count)
    flops = 6 * total * width * hidden_width
    half_count = expert_count // 2
    forward, waiting = [], pieces[half_count:]
    for half_pieces in (pieces[:half_count], None):
        forward.append(
            list(expert_call(
                functools.partial(forward_kernel, rows, half_count, expert_count),
                [half_wide] + [half_narrow] * 3,
                [half_wide, ((total // 2, side), bf16)] + [half_narrow] * 3 + [half_wide],
                [half_count, half_count, 5],
                flops // 2,
                [where, *(half_pieces or waiting), *weights],
            ))
        )
        if half_pieces:
            forward[0][0], waiting = tie((forward[0][0], waiting))
    (out_keep, out_send), gate_pre, up_pre, hidden = zip(*forward)
    held = [wide, ((total, side), bf16), narrow, narrow]
    out_came = swap_inner(out_send, SECOND)
    rows_in, hidden = pl.pallas_call(
        functools.partial(assemble_kernel, rows, expert_count),
        out_shape=[jax.ShapeDtypeStruct(*wide), jax.ShapeDtypeStruct(*narrow)],
        in_specs=[ANY] * (expert_count + 2),
        out_specs=[ANY, ANY],
        scratch_shapes=[
            pltpu.VMEM(*wide),
            pltpu.VMEM(*narrow),
            pltpu.SemaphoreType.DMA((expert_count,)),
            pltpu.SemaphoreType.DMA((2,)),
            pltpu.SemaphoreType.DMA((2,)),
        ],
        compiler_params=pltpu.CompilerParams(vmem_limit_bytes=VMEM_LIMIT // 4),
    )(*in_hbm(pieces), *in_hbm(hidden))
    grad_keep, grad_send, dgate, dup, rows_scaled = expert_call(
        functools.partial(backward_kernel, rows, expert_count),
        [half_wide, half_wide, narrow, narrow, wide],
        held + [narrow, narrow, wide],
        [expert_count, expert_count, 4, 7],
        flops,
        [where, *gate_pre, *up_pre, *pieces, *weights],
    )
    grad_came = swap_inner(grad_send, SECOND)
    out_column = reduce_part(out_keep.reshape(2, -1, width), out_came)
    grad_came, out_column, dgate, dup, rows_scaled, hidden, rows_in = tie(
        (grad_came, out_column, dgate, dup, rows_scaled, hidden, rows_in)
    )

    def half(value, which, size):
        return lax.dynamic_slice_in_dim(value, which * size, size, 1)

    other = 1 - replica
    sent = (
        contract_rows(half(rows_in, other, half_width), dgate).astype(bf16),
        contract_rows(half(rows_in, other, half_width), dup).astype(bf16),
        contract_rows(half(hidden, other, half_hidden), rows_scaled).astype(bf16),
    )
    back = partner_2(sent, "rep", 0)
    gate_out = add_bf16(contract_rows(half(rows_in, replica, half_width), dgate), back[0])
    up_out = add_bf16(contract_rows(half(rows_in, replica, half_width), dup), back[1])
    down_out = add_bf16(contract_rows(half(hidden, replica, half_hidden), rows_scaled), back[2])
    masks = [2**bit for bit in range(lax.axis_size("grp").bit_length() - 1)]
    out_column = halve_column(out_column, masks[:-1])
    half = out_column.shape[0] // 2
    out_terms = [out_column[:half], swap_group(out_column[half:], masks[-1])]
    grad_column = reduce_part(grad_keep.reshape(2, -1, width), grad_came)
    grad_terms = send_column(grad_column)
    out_terms, grad_terms[1], gate_out, up_out, down_out = tie(
        (out_terms, grad_terms[1], gate_out, up_out, down_out)
    )
    layer_out, token_grad = add_all(out_terms), add_all(grad_terms)
    return layer_out, token_grad, gate_out[None], up_out[None], down_out[None]


def solution(mesh):
    in_specs = (
        P(("grp", "exp", "rep"), None),
        P(("grp", "exp", "rep"), None),
        P(("grp", "exp", "rep"), None),
        P(("grp", "exp", "rep"), None),
        P(("grp", "exp"), "rep", None),
        P(("grp", "exp"), "rep", None),
        P(("grp", "exp"), "rep", None),
    )
    out_specs = (
        P(("grp", "exp", "rep"), None),
        P(("grp", "exp", "rep"), None),
        P(("grp", "exp"), "rep", None),
        P(("grp", "exp"), "rep", None),
        P(("grp", "exp"), "rep", None),
    )
    sizes = dict(mesh.shape)
    group_bits = sizes["grp"] & (sizes["grp"] - 1) == 0
    whole_blocks = sizes["exp"] == 4 and sizes["rep"] == 2 and group_bits and sizes["grp"] * sizes["exp"] <= 2 * TOP
    local = dense_local if whole_blocks else routed_local
    return jax.shard_map(local, mesh=mesh, in_specs=in_specs, out_specs=out_specs, check_vma=False)
```
